512 devices in a mesh: segment: 8 (over x, core), dev: 64 (over z, y).
Axes of the slice: x: 4, y: 8, z: 8, core: 2. Of those that a mesh axis runs over, the one named last changes fastest.
Arguments:
- queries: bfloat16 [512, 8192], P(('segment', 'dev')), may hold values from -64 to 64
- page_ids: int32 [512, 4, 32], P(('segment', 'dev')), may hold values from 0 to 1023, as said below
- key_pages: bfloat16 [8192, 64, 128], P(('segment', 'dev')), may hold values from -6 to 6
- value_pages: bfloat16 [8192, 64, 128], P(('segment', 'dev')), may hold values from -6 to 6
- out_weight: bfloat16 [65536, 16384], P(('segment', 'dev')), may hold values from -0.1875 to 0.1875
Outputs:
- block_out: bfloat16 [512, 16384], P(('segment', 'dev'))
The draws below stay inside these ranges and needn't reach their ends.
Inputs may be any that keep to these rules, and one draw needn't show every extreme that they name: `page_ids`: within the rows of one device (aligned blocks of 1 row), at most 4 of the entries name pages of one device (id // 16); in every section one such device, the same for all of its row blocks, is named exactly 4 times from each block. The 32 ids of one row and key head are distinct.
All inputs are finite; a program needn't handle non-finite values.
Results may differ from the reference program's by a relative error of at most 0.006.
Values may be sent and summed in bfloat16 or wider, within the bound.
No kernel may reach another device: no remote copies, remote signals or barrier semaphores. Data moves between devices by JAX's collectives and lax.ppermute only.
A program may use at most 64 MiB of HBM per device.

```python
import math
import jax
import jax.numpy as jnp
from jax import lax

D = 16384
HQ = 64
KVH = 4
HD = 128
PAGE = 64
SEL = 32
ROWS_DEV = 1
PAGES_DEV = 16
GROUP = 16
R_SEC = 64
ROWS = 512
PAGES = 1024
N_SEGMENT = 8
N_DEV = 64


def draw_queries(key, part):
    array_shape = (ROWS, HQ * HD)
    drawn = jnp.clip(2.0 * jax.random.normal(jax.random.fold_in(key, 12), array_shape, jnp.float32), -8.0, 8.0)
    return drawn.astype(jnp.bfloat16)


def draw_key_pages(key, part):
    array_shape = (N_SEGMENT * PAGES, PAGE, HD)
    drawn = jnp.clip(jax.random.normal(jax.random.fold_in(key, 22), array_shape, jnp.float32), -6.0, 6.0)
    return drawn.astype(jnp.bfloat16)


def draw_page_ids(key, part):
    per_block = ROWS_DEV * KVH * SEL
    blocks = ROWS // ROWS_DEV
    capacity = 2 * per_block // N_DEV
    position = jnp.arange(per_block, dtype=jnp.int32)
    hot_section = jax.random.randint(jax.random.fold_in(key, 31), (blocks // N_DEV,), 0, N_DEV, dtype=jnp.int32)
    hot_block = jnp.repeat(hot_section, N_DEV)[:, None]
    others = (hot_block + 1 + (position[None, :] - capacity) % (N_DEV - 1)) % N_DEV
    owners = jnp.where(position[None, :] < capacity, hot_block, others)
    block_keys = jax.random.split(jax.random.fold_in(key, 32), blocks)
    orders = jax.vmap(lambda one_key: jax.random.permutation(one_key, per_block))(block_keys)
    owners = jnp.take_along_axis(owners, orders.astype(jnp.int32), axis=1)
    owners = owners.reshape(ROWS * KVH, SEL)
    chosen_index = jnp.arange(SEL, dtype=jnp.int32)
    matches = (owners[:, :, None] == owners[:, None, :]) & (chosen_index[None, None, :] < chosen_index[None, :, None])
    rank_ids = jnp.sum(matches.astype(jnp.int32), axis=2)
    offsets = jax.random.randint(jax.random.fold_in(key, 33), (ROWS * KVH, 1), 0, PAGES_DEV, dtype=jnp.int32)
    slot_ids = (offsets + rank_ids) % PAGES_DEV
    return (owners * PAGES_DEV + slot_ids).reshape(ROWS, KVH, SEL).astype(jnp.int32)


def steps_of(key, dims, cuts, low, top_value):
    loudness = 1.0
    for dim, parts in cuts:
        draws = jax.random.uniform(jax.random.fold_in(jax.random.fold_in(key, 6), dim), (parts,), jnp.float32, low / len(cuts), top_value / len(cuts))
        loudness = loudness * jnp.repeat(jnp.exp(draws), dims[dim] // parts).reshape((-1,) + (1,) * (len(dims) - 1 - dim))
    return loudness


def bell_draw(rng, extent, scale, bound, cuts=(), kind=jnp.bfloat16):
    array = scale * jax.random.normal(rng, extent, jnp.float32)
    if cuts:
        array = array * steps_of(rng, extent, cuts, -0.22, 0.18)
    return jnp.clip(array, -bound, bound).astype(kind)


def setup_inputs(seed: int = 0) -> dict:
    arg_keys = jax.random.split(jax.random.key(seed), 6)
    return {
        "queries": draw_queries(jax.random.fold_in(arg_keys[5], 71), 0),
        "page_ids": draw_page_ids(jax.random.fold_in(arg_keys[5], 71), 0),
        "key_pages": draw_key_pages(jax.random.fold_in(arg_keys[5], 71), 0),
        "value_pages": bell_draw(arg_keys[3], (N_SEGMENT * PAGES, PAGE, HD), 1.0, 6.0, ((0, 512),)),
        "out_weight": bell_draw(arg_keys[4], (N_SEGMENT * HQ * HD, D), (HQ * HD // 8) ** -0.5, 0.1875, ((0, 512),)),
    }


def section_rows(query_rows, id_rows, key_pool, value_pool):
    score_scale = 1.0 / math.sqrt(HD)

    def one_row(row_pair):
        query_row, id_row = row_pair
        query_heads = query_row.reshape(KVH, GROUP, HD).astype(jnp.float32)
        page_keys = key_pool[id_row].astype(jnp.float32)
        page_values = value_pool[id_row].astype(jnp.float32)
        scores = jnp.einsum('kgd,kptd->kgpt', query_heads, page_keys) * score_scale
        page_max = lax.optimization_barrier(jnp.max(scores, axis=-1))
        rounded = jnp.exp(scores - page_max[..., None]).astype(jnp.bfloat16)
        weights = lax.optimization_barrier(rounded).astype(jnp.float32)
        weight_sum = lax.optimization_barrier(jnp.sum(weights, axis=-1))
        partial_value = jnp.einsum('kgpt,kptd->kgpd', weights, page_values)
        highest = lax.optimization_barrier(jnp.max(page_max, axis=-1, keepdims=True))
        factor = jnp.exp(page_max - highest)
        numerator = lax.optimization_barrier(jnp.sum(factor[..., None] * partial_value, axis=2))
        denominator = lax.optimization_barrier(jnp.sum(factor * weight_sum, axis=2))
        attended = numerator / denominator[..., None]
        return attended.reshape(-1).astype(jnp.bfloat16)
    return lax.map(one_row, (query_rows, id_rows))

def reference(queries, page_ids, key_pages, value_pages, out_weight):
    head_width = HQ * HD
    outputs = []
    for section in range(N_SEGMENT):
        row_lo = section * R_SEC
        page_lo = section * PAGES
        attended = section_rows(queries[row_lo:row_lo + R_SEC], page_ids[row_lo:row_lo + R_SEC], key_pages[page_lo:page_lo + PAGES], value_pages[page_lo:page_lo + PAGES])
        weight_rows = out_weight[section * head_width:(section + 1) * head_width]
        projected = jnp.dot(attended, weight_rows, preferred_element_type=jnp.float32).astype(jnp.bfloat16)
        outputs.append(projected)
    return jnp.roll(jnp.concatenate(outputs, axis=0), R_SEC, axis=0)
```

```python
import math

import jax
import jax.numpy as jnp
from jax import lax
from jax.experimental import pallas as pl
from jax.experimental.pallas import tpu as pltpu
from jax.sharding import PartitionSpec as P

BF = jnp.bfloat16
F32 = jnp.float32
HEADS = 64
GROUP = 16
KVH = 4
HD = 128
ROWS = 64
POOL = 16
TOKENS = 1024
SLAB = 72
BLOCK = 2048
LOG2E = math.log2(math.e)
SCALE = 1.0 / math.sqrt(HD)
FAR = float(2**20)
FLOOR = -8192.0


def iota(shape, dim):
    return lax.broadcasted_iota(jnp.int32, shape, dim)


def dot(a, b):
    return lax.dot_general(a, b, (((1,), (0,)), ((), ())), preferred_element_type=F32)


def dot_nt(a, b):
    return lax.dot_general(a, b, (((1,), (1,)), ((), ())), preferred_element_type=F32)


def one_if(condition):
    return jnp.where(condition, 1.0, 0.0).astype(BF)


def attend_kernel(me_ref, q_ref, k_ref, v_ref, out_ref, qs, kaug, vt, bias):
    me = me_ref[0].astype(F32)
    i, j = iota((256, 256), 0), iota((256, 256), 1)
    swap = one_if((j % 16) * 16 + j // 16 == i)
    for h in range(KVH):
        for c in range(4):
            part = q_ref[c * 16 : (c + 1) * 16, h * 16 : (h + 1) * 16, :]
            turned = dot(swap, part.reshape(256, HD)).astype(BF)
            for g in range(GROUP):
                row = (h * GROUP + g) * ROWS + c * 16
                qs[row : row + 16, :] = turned[g * 16 : (g + 1) * 16, :]
    i, j = iota((HD, HD), 0), iota((HD, HD), 1)
    vt[0:HD, :] = dot_nt(one_if(i == j), v_ref[...]).astype(BF)
    vt[HD : HD + 16, :] = jnp.ones((16, TOKENS), BF)
    token, lane = iota((TOKENS, HD), 0), iota((TOKENS, HD), 1)
    for h in range(KVH):
        kaug[h, :, 0:HD] = k_ref[...]
        kaug[h, :, HD : 2 * HD] = one_if(lane == h * POOL + token // 64)
    ids = q_ref[:, HEADS:SLAB, :].astype(F32).reshape(ROWS * 8, HD).astype(BF)
    i, j = iota((ROWS, ROWS * 8), 0), iota((ROWS, ROWS * 8), 1)
    owner = dot(one_if(j == i * 8), ids)
    slot = dot(one_if(j == i * 8 + 1), ids)
    slot = jnp.where(owner == me, slot, -1.0)
    i, j = iota((HD, HD), 0), iota((HD, HD), 1)
    count = jnp.zeros((ROWS, HD), F32)
    for page in range(POOL):
        count += dot(one_if(slot == float(page)), one_if(j == (i // 32) * POOL + page))
    bias[...] = jnp.where(count > 0.5, 0.0, -FAR).astype(BF)

    low = iota((1, HD), 1) < 64
    row8 = iota((8, HD), 0)

    def step(n, carry):
        h = n // 4
        q = qs[pl.ds(pl.multiple_of(n * 256, 256), 256), :]
        b = bias[...]
        qa = jnp.concatenate([q, jnp.concatenate([b, b, b, b], axis=0)], axis=1)
        s = dot_nt(kaug[h], qa)
        top = jnp.max(s, axis=0, keepdims=True) * SCALE
        point = jnp.maximum(top.astype(BF).astype(F32), FLOOR)
        p = jnp.exp2(s * (SCALE * LOG2E) - point * LOG2E).astype(BF)
        o = dot(vt[...], p)
        for pair in range(2):
            lanes = slice(pair * 128, (pair + 1) * 128)
            lo, hi = o[0:64, lanes], o[64:128, lanes]
            lo_turned, hi_turned = pltpu.roll(lo, 64, 1), pltpu.roll(hi, 64, 1)
            total = o[HD : HD + 1, lanes]
            total_hi = total.astype(BF).astype(F32)
            stats = jnp.where(
                row8 == 0,
                point[:, lanes],
                jnp.where(row8 == 1, total_hi, total - total_hi),
            )
            stats_turned = pltpu.roll(stats, 64, 1)
            head = n * 4 + pair * 2
            out_ref[head, 0:64, :] = jnp.where(low, lo, hi_turned).astype(BF)
            out_ref[head, 64:SLAB, :] = jnp.where(low, stats, stats_turned).astype(BF)
            out_ref[head + 1, 0:64, :] = jnp.where(low, lo_turned, hi).astype(BF)
            out_ref[head + 1, 64:SLAB, :] = jnp.where(low, stats_turned, stats).astype(BF)
        return carry

    lax.fori_loop(0, 16, step, 0)


def project_kernel(r_ref, w_ref, out_ref, att, tmp):
    @pl.when(pl.program_id(0) == 0)
    def _():
        stats = r_ref[:, 64:SLAB, :].astype(F32)
        top = jnp.max(stats, axis=0)
        factor = jnp.exp2((stats - top[None]) * LOG2E)
        den = jnp.zeros((1, HD), F32)
        acc = jnp.zeros((64, HD), F32)
        for src in range(ROWS):
            f = factor[src, 0:1, :]
            den += f * (stats[src, 1:2, :] + stats[src, 2:3, :])
            acc += f * r_ref[src, 0:64, :].astype(F32)
        both = acc / den
        tall = jnp.concatenate([both, pltpu.roll(both, 64, 1)], axis=0)
        att[...] = tall.T[0:ROWS, :].astype(BF)

    x = dot(att[...], w_ref[...])
    for cb in range(BLOCK // 128):
        tmp[pl.ds(cb, ROWS, stride=BLOCK // 128), :] = x[:, cb * 128 : (cb + 1) * 128]
    out_ref[...] = tmp[...].reshape(ROWS, BLOCK // 128, 128).astype(BF)


def attend(me, got, keys, values):
    return pl.pallas_call(
        attend_kernel,
        out_shape=jax.ShapeDtypeStruct((HEADS, SLAB, HD), BF),
        in_specs=[pl.BlockSpec(memory_space=pltpu.SMEM)] + [pl.BlockSpec(memory_space=pltpu.VMEM)] * 3,
        out_specs=pl.BlockSpec(memory_space=pltpu.VMEM),
        scratch_shapes=[
            pltpu.VMEM((HEADS * ROWS, HD), BF),
            pltpu.VMEM((KVH, TOKENS, 2 * HD), BF),
            pltpu.VMEM((HD + 16, TOKENS), BF),
            pltpu.VMEM((ROWS, HD), BF),
        ],
        compiler_params=pltpu.CompilerParams(vmem_limit_bytes=32 * 2**20),
        name="attend",
    )(me, got, keys, values)


def project(merged, weight):
    width = weight.shape[1]
    return pl.pallas_call(
        project_kernel,
        out_shape=jax.ShapeDtypeStruct((ROWS, width // 128, 128), BF),
        grid=(width // BLOCK,),
        in_specs=[
            pl.BlockSpec((ROWS, SLAB, HD), lambda n: (0, 0, 0)),
            pl.BlockSpec((HD, BLOCK), lambda n: (0, n)),
        ],
        out_specs=pl.BlockSpec((ROWS, BLOCK // 128, 128), lambda n: (0, n, 0)),
        scratch_shapes=[pltpu.VMEM((ROWS, HD), BF), pltpu.VMEM((ROWS * BLOCK // 128, 128), F32)],
        compiler_params=pltpu.CompilerParams(vmem_limit_bytes=32 * 2**20),
        name="project",
    )(merged, weight)


def exchange(value):
    return lax.all_to_all(value, "dev", split_axis=0, concat_axis=0, tiled=True)


def local(queries, page_ids, key_pages, value_pages, out_weight):
    count = lax.axis_size("segment")
    ids = page_ids.reshape(1, KVH * page_ids.shape[2])
    payload = jnp.concatenate(
        [
            queries.reshape(HEADS, HD),
            (ids // POOL).astype(BF),
            (ids % POOL).astype(BF),
            jnp.zeros((SLAB - HEADS - 2, HD), BF),
        ],
        axis=0,
    )
    got = exchange(jnp.broadcast_to(payload[None], (ROWS, SLAB, HD)))
    me = lax.axis_index("dev").astype(jnp.int32).reshape(1)
    partial = attend(me, got, key_pages.reshape(TOKENS, HD), value_pages.reshape(TOKENS, HD))
    sums = project(exchange(partial), out_weight)
    parts = exchange(sums)
    projected = jnp.sum(parts.astype(F32), axis=0).astype(BF)
    handed = lax.ppermute(projected, "segment", [(s, (s + 1) % count) for s in range(count)])
    return handed.reshape(1, -1)


def solution(mesh):
    placed = (
        P(("segment", "dev"), None),
        P(("segment", "dev"), None, None),
        P(("segment", "dev"), None, None),
        P(("segment", "dev"), None, None),
        P(("segment", "dev"), None),
    )
    return jax.shard_map(
        local, mesh=mesh, in_specs=placed, out_specs=P(("segment", "dev"), None), check_vma=False
    )
```

```python
import math

import jax
import jax.numpy as jnp
from jax import lax
from jax.experimental import pallas as pl
from jax.experimental.pallas import tpu as pltpu
from jax.sharding import PartitionSpec as P

BF = jnp.bfloat16
F32 = jnp.float32
HEADS = 64
GROUP = 16
KVH = 4
HD = 128
ROWS = 64
POOL = 16
TOKENS = 1024
SLAB = 72
BLOCK = 2048
CHUNK = 1024
LOG2E = math.log2(math.e)
SCALE = 1.0 / math.sqrt(HD)
FAR = float(2**20)
FLOOR = -8192.0


def iota(shape, dim):
    return lax.broadcasted_iota(jnp.int32, shape, dim)


def dot(a, b):
    return lax.dot_general(a, b, (((1,), (0,)), ((), ())), preferred_element_type=F32)


def dot_nt(a, b):
    return lax.dot_general(a, b, (((1,), (1,)), ((), ())), preferred_element_type=F32)


def one_if(condition):
    return jnp.where(condition, 1.0, 0.0).astype(BF)


def attend_kernel(me_ref, q_ref, k_ref, v_ref, out_ref, qs, kaug, vt, bias):
    me = me_ref[0].astype(F32)
    i, j = iota((256, 256), 0), iota((256, 256), 1)
    swap = one_if((j % 16) * 16 + j // 16 == i)
    for h in range(KVH):
        for c in range(4):
            part = q_ref[c * 16 : (c + 1) * 16, h * 16 : (h + 1) * 16, :]
            turned = dot(swap, part.reshape(256, HD)).astype(BF)
            for g in range(GROUP):
                row = (h * GROUP + g) * ROWS + c * 16
                qs[row : row + 16, :] = turned[g * 16 : (g + 1) * 16, :]
    vt[:, 0:HD] = v_ref[...]
    vt[:, HD : 2 * HD] = one_if(iota((TOKENS, HD), 1) == 0)
    token, lane = iota((TOKENS, HD), 0), iota((TOKENS, HD), 1)
    for h in range(KVH):
        kaug[h, :, 0:HD] = k_ref[...]
        kaug[h, :, HD : 2 * HD] = one_if(lane == h * POOL + token // 64)
    ids = q_ref[:, HEADS:SLAB, :].astype(F32).reshape(ROWS * 8, HD).astype(BF)
    i, j = iota((ROWS, ROWS * 8), 0), iota((ROWS, ROWS * 8), 1)
    owner = dot(one_if(j == i * 8), ids)
    slot = dot(one_if(j == i * 8 + 1), ids)
    slot = jnp.where(owner == me, slot, -1.0)
    i, j = iota((HD, HD), 0), iota((HD, HD), 1)
    count = jnp.zeros((ROWS, HD), F32)
    for page in range(POOL):
        count += dot(one_if(slot == float(page)), one_if(j == (i // 32) * POOL + page))
    bias[...] = jnp.where(count > 0.5, 0.0, -FAR).astype(BF)

    low = iota((1, HD), 1) < 64
    row8 = iota((8, HD), 0)
    lane = iota((CHUNK, HD), 1)
    per = CHUNK // ROWS

    def step(n, carry):
        h = n * per // GROUP
        q = qs[pl.ds(pl.multiple_of(n * CHUNK, CHUNK), CHUNK), :]
        b = bias[...]
        qa = jnp.concatenate([q, jnp.concatenate([b] * per, axis=0)], axis=1)
        s = dot_nt(qa, kaug[h])
        top = jnp.max(s, axis=1, keepdims=True) * SCALE
        point = jnp.maximum(top.astype(BF).astype(F32), FLOOR)
        p = jnp.exp2(s * (SCALE * LOG2E) - point * LOG2E).astype(BF)
        o = dot(p, vt[...])
        total = o[:, HD : HD + 1]
        total_hi = total.astype(BF).astype(F32)
        stats = jnp.where(lane == 0, point, jnp.where(lane == 1, total_hi, total - total_hi))
        ot = o[:, 0:HD].T
        st = stats.T
        for pair in range(per // 2):
            lanes = slice(pair * 128, (pair + 1) * 128)
            lo, hi = ot[0:64, lanes], ot[64:128, lanes]
            lo_turned, hi_turned = pltpu.roll(lo, 64, 1), pltpu.roll(hi, 64, 1)
            stats = st[0:8, lanes]
            stats_turned = pltpu.roll(stats, 64, 1)
            head = n * per + pair * 2
            out_ref[head, 0:64, :] = jnp.where(low, lo, hi_turned).astype(BF)
            out_ref[head, 64:SLAB, :] = jnp.where(low, stats, stats_turned).astype(BF)
            out_ref[head + 1, 0:64, :] = jnp.where(low, lo_turned, hi).astype(BF)
            out_ref[head + 1, 64:SLAB, :] = jnp.where(low, stats_turned, stats).astype(BF)
        return carry

    lax.fori_loop(0, HEADS * ROWS // CHUNK, step, 0)


def project_kernel(r_ref, w_ref, out_ref, att, tmp):
    @pl.when(pl.program_id(0) == 0)
    def _():
        stats = r_ref[:, 64:SLAB, :].astype(F32)
        top = jnp.max(stats, axis=0)
        factor = jnp.exp2((stats - top[None]) * LOG2E)
        den = jnp.zeros((1, HD), F32)
        acc = jnp.zeros((64, HD), F32)
        for src in range(ROWS):
            f = factor[src, 0:1, :]
            den += f * (stats[src, 1:2, :] + stats[src, 2:3, :])
            acc += f * r_ref[src, 0:64, :].astype(F32)
        both = acc / den
        tall = jnp.concatenate([both, pltpu.roll(both, 64, 1)], axis=0)
        att[...] = tall.T[0:ROWS, :].astype(BF)

    x = dot(att[...], w_ref[...])
    for cb in range(BLOCK // 128):
        tmp[pl.ds(cb, ROWS, stride=BLOCK // 128), :] = x[:, cb * 128 : (cb + 1) * 128]
    out_ref[...] = tmp[...].reshape(ROWS, BLOCK // 128, 128).astype(BF)


def attend(me, got, keys, values):
    return pl.pallas_call(
        attend_kernel,
        out_shape=pltpu.HBM((HEADS, SLAB, HD), BF),
        in_specs=[pl.BlockSpec(memory_space=pltpu.SMEM)] + [pl.BlockSpec(memory_space=pltpu.VMEM)] * 3,
        out_specs=pl.BlockSpec(memory_space=pltpu.VMEM),
        scratch_shapes=[
            pltpu.VMEM((HEADS * ROWS, HD), BF),
            pltpu.VMEM((KVH, TOKENS, 2 * HD), BF),
            pltpu.VMEM((TOKENS, 2 * HD), BF),
            pltpu.VMEM((ROWS, HD), BF),
        ],
        compiler_params=pltpu.CompilerParams(vmem_limit_bytes=32 * 2**20),
        name="attend",
    )(me, got, keys, values)


def project(merged, weight):
    width = weight.shape[1]
    return pl.pallas_call(
        project_kernel,
        out_shape=pltpu.HBM((ROWS, width // 128, 128), BF),
        grid=(width // BLOCK,),
        in_specs=[
            pl.BlockSpec((ROWS, SLAB, HD), lambda n: (0, 0, 0)),
            pl.BlockSpec((HD, BLOCK), lambda n: (0, n)),
        ],
        out_specs=pl.BlockSpec((ROWS, BLOCK // 128, 128), lambda n: (0, n, 0)),
        scratch_shapes=[pltpu.VMEM((ROWS, HD), BF), pltpu.VMEM((ROWS * BLOCK // 128, 128), F32)],
        compiler_params=pltpu.CompilerParams(vmem_limit_bytes=32 * 2**20),
        name="project",
    )(merged, weight)


def exchange(value):
    return lax.all_to_all(value, "dev", split_axis=0, concat_axis=0, tiled=True)


def local(queries, page_ids, key_pages, value_pages, out_weight):
    count = lax.axis_size("segment")
    ids = page_ids.reshape(1, KVH * page_ids.shape[2])
    payload = jnp.concatenate(
        [
            queries.reshape(HEADS, HD),
            (ids // POOL).astype(BF),
            (ids % POOL).astype(BF),
            jnp.zeros((SLAB - HEADS - 2, HD), BF),
        ],
        axis=0,
    )
    got = exchange(jnp.broadcast_to(payload[None], (ROWS, SLAB, HD)))
    me = lax.axis_index("dev").astype(jnp.int32).reshape(1)
    partial = attend(me, got, key_pages.reshape(TOKENS, HD), value_pages.reshape(TOKENS, HD))
    sums = project(exchange(partial), out_weight)
    parts = exchange(sums)
    projected = jnp.sum(parts.astype(F32), axis=0).astype(BF)
    handed = lax.ppermute(projected, "segment", [(s, (s + 1) % count) for s in range(count)])
    return handed.reshape(1, -1)


def solution(mesh):
    placed = (
        P(("segment", "dev"), None),
        P(("segment", "dev"), None, None),
        P(("segment", "dev"), None, None),
        P(("segment", "dev"), None, None),
        P(("segment", "dev"), None),
    )
    return jax.shard_map(
        local, mesh=mesh, in_specs=placed, out_specs=P(("segment", "dev"), None), check_vma=False
    )
```

```python
import math

import jax
import jax.numpy as jnp
from jax import lax
from jax.experimental import pallas as pl
from jax.experimental.pallas import tpu as pltpu
from jax.sharding import PartitionSpec as P

BF = jnp.bfloat16
F32 = jnp.float32
HEADS = 64
GROUP = 16
KVH = 4
HD = 128
ROWS = 64
POOL = 16
TOKENS = 1024
SLAB = 72
PAGE = 64
SEL = 32
LINE = 8
BLOCK = 4096
CHUNK = 1024
LOG2E = math.log2(math.e)
SCALE = 1.0 / math.sqrt(HD)
FAR = float(2**20)
FLOOR = -8192.0


def iota(shape, dim):
    return lax.broadcasted_iota(jnp.int32, shape, dim)


def dot(a, b):
    return lax.dot_general(a, b, (((1,), (0,)), ((), ())), preferred_element_type=F32)


def dot_nt(a, b):
    return lax.dot_general(a, b, (((1,), (1,)), ((), ())), preferred_element_type=F32)


def one_if(condition):
    return jnp.where(condition, 1.0, 0.0).astype(BF)


def prepare_kernel(q_ref, id_ref, out_ref, tmp):
    for head in range(HEADS):
        tmp[head : head + 1, :] = q_ref[:, head * HD : (head + 1) * HD].astype(F32)
    ids = id_ref[...]
    tmp[HEADS:SLAB, :] = jnp.full((SLAB - HEADS, HD), -1.0, F32)
    tmp[HEADS : HEADS + KVH, 0:SEL] = (ids // POOL).astype(F32)
    tmp[HEADS + KVH : SLAB, 0:SEL] = (ids % POOL).astype(F32)
    slab = tmp[...].astype(BF)
    for copy in range(LINE):
        out_ref[copy, :, :] = slab


def attend_kernel(where_ref, q_ref, k_ref, v_ref, out_ref, qs, bias):
    me = where_ref[0].astype(F32)
    odd = where_ref[1]
    i, j = iota((256, 256), 0), iota((256, 256), 1)
    swap = one_if((j % 16) * 16 + j // 16 == i)
    for h in range(KVH):
        for c in range(4):
            part = q_ref[c * 16 : (c + 1) * 16, h * 16 : (h + 1) * 16, :]
            turned = dot(swap, part.reshape(256, HD)).astype(BF)
            for g in range(GROUP):
                row = (h * GROUP + g) * ROWS + c * 16
                qs[row : row + 16, :] = turned[g * 16 : (g + 1) * 16, :]
    ids = q_ref[:, HEADS:SLAB, :].astype(F32).reshape(ROWS * 8, HD).astype(BF)
    i, j = iota((KVH * ROWS, ROWS * 8), 0), iota((KVH * ROWS, ROWS * 8), 1)
    first = (i % ROWS) * 8 + i // ROWS
    owner = dot(one_if(j == first), ids)
    slot = dot(one_if(j == first + KVH), ids)
    slot = jnp.where(owner == me, slot, -1.0)
    j = iota((HD, HD), 1)
    count = jnp.zeros((KVH * ROWS, HD), F32)
    for page in range(POOL):
        count += dot(one_if(slot == float(page)), one_if(j == page))
    bias[...] = jnp.where(count > 0.5, 0.0, -FAR).astype(BF)

    low = iota((1, HD), 1) < 64
    lane = iota((CHUNK, HD), 1)
    per = CHUNK // ROWS
    page_of = one_if(iota((TOKENS, HD), 1) == iota((TOKENS, HD), 0) // PAGE)
    first_lane = one_if(iota((TOKENS, HD), 1) == 0)

    def step(n, carry):
        h = n * per // GROUP
        q = qs[pl.ds(pl.multiple_of(n * CHUNK, CHUNK), CHUNK), :]
        b = bias[pl.ds(pl.multiple_of(h * ROWS, ROWS), ROWS), :]
        qa = jnp.concatenate([q, jnp.concatenate([b] * per, axis=0)], axis=1)
        s = dot_nt(qa, jnp.concatenate([k_ref[...], page_of], axis=1))
        top = jnp.max(s, axis=1, keepdims=True) * SCALE
        point = jnp.maximum(top.astype(BF).astype(F32), FLOOR)
        p = jnp.exp2(s * (SCALE * LOG2E) - point * LOG2E).astype(BF)
        o = dot(p, jnp.concatenate([v_ref[...], first_lane], axis=1))
        total = o[:, HD : HD + 1]
        total_hi = total.astype(BF).astype(F32)
        stats = jnp.where(lane == 0, point, jnp.where(lane == 1, total_hi, total - total_hi))
        ot = o[:, 0:HD].T
        st = stats.T
        for pair in range(per // 2):
            lanes = slice(pair * 128, (pair + 1) * 128)
            lo, hi = ot[0:64, lanes], ot[64:128, lanes]
            lo_turned, hi_turned = pltpu.roll(lo, 64, 1), pltpu.roll(hi, 64, 1)
            stats = st[0:8, lanes]
            stats_turned = pltpu.roll(stats, 64, 1)
            head = n * per + pair * 2
            swapped = (head % LINE) * LINE + head // LINE
            even_at = jnp.where(odd == 1, head, swapped)
            odd_at = jnp.where(odd == 1, head + 1, swapped + LINE)
            out_ref[even_at, 0:64, :] = jnp.where(low, lo, hi_turned).astype(BF)
            out_ref[even_at, 64:SLAB, :] = jnp.where(low, stats, stats_turned).astype(BF)
            out_ref[odd_at, 0:64, :] = jnp.where(low, lo_turned, hi).astype(BF)
            out_ref[odd_at, 64:SLAB, :] = jnp.where(low, stats_turned, stats).astype(BF)
        return carry

    lax.fori_loop(0, HEADS * ROWS // CHUNK, step, 0)


def merged(slab_of):
    stats = [slab_of(src, slice(64, SLAB)).astype(F32) for src in range(LINE)]
    points = [s[0:1, :] for s in stats]
    top = points[0]
    for point in points[1:]:
        top = jnp.maximum(top, point)
    total = jnp.zeros((1, HD), F32)
    acc = jnp.zeros((64, HD), F32)
    for src in range(LINE):
        f = jnp.exp2((points[src] - top) * LOG2E)
        total += f * (stats[src][1:2, :] + stats[src][2:3, :])
        acc += f * slab_of(src, slice(0, 64)).astype(F32)
    return top, total, acc


def merge_kernel(r_ref, out_ref):
    row8 = iota((8, HD), 0)
    for head in range(LINE):
        top, total, acc = merged(lambda src, rows: r_ref[src, head, rows, :])
        total_hi = total.astype(BF).astype(F32)
        stats = jnp.where(row8 == 0, top, jnp.where(row8 == 1, total_hi, total - total_hi))
        out_ref[head, 0:64, :] = acc.astype(BF)
        out_ref[head, 64:SLAB, :] = stats.astype(BF)


def project_kernel(r_ref, w_ref, out_ref, att):
    @pl.when(pl.program_id(0) == 0)
    def _():
        top, total, acc = merged(lambda src, rows: r_ref[src, rows, :])
        both = acc / total
        tall = jnp.concatenate([both, pltpu.roll(both, 64, 1)], axis=0)
        att[...] = tall.T[0:ROWS, :].astype(BF)

    out_ref[...] = dot(att[...], w_ref[...]).astype(BF)


def add_kernel(x_ref, out_ref, tmp):
    tiles = tmp.shape[0] // LINE
    for tile in range(tiles):
        total = x_ref[0, :, tile * 128 : (tile + 1) * 128].astype(F32)
        for src in range(1, LINE):
            total += x_ref[src, :, tile * 128 : (tile + 1) * 128].astype(F32)
        tmp[pl.ds(tile, LINE, stride=tiles), :] = total
    out_ref[...] = tmp[...].reshape(LINE, tiles, 128).astype(BF)


VMEM = pl.BlockSpec(memory_space=pltpu.VMEM)
SMEM = pl.BlockSpec(memory_space=pltpu.SMEM)
PARAMS = pltpu.CompilerParams(vmem_limit_bytes=40 * 2**20)


def prepare(queries, ids):
    return pl.pallas_call(
        prepare_kernel,
        out_shape=jax.ShapeDtypeStruct((LINE, SLAB, HD), BF),
        in_specs=[VMEM, VMEM],
        out_specs=VMEM,
        scratch_shapes=[pltpu.VMEM((SLAB, HD), F32)],
        compiler_params=PARAMS,
        name="prepare",
    )(queries, ids)


def attend(place, got, keys, values):
    return pl.pallas_call(
        attend_kernel,
        out_shape=jax.ShapeDtypeStruct((HEADS, SLAB, HD), BF),
        in_specs=[SMEM, VMEM, VMEM, VMEM],
        out_specs=VMEM,
        scratch_shapes=[pltpu.VMEM((HEADS * ROWS, HD), BF), pltpu.VMEM((KVH * ROWS, HD), BF)],
        compiler_params=PARAMS,
        name="attend",
    )(place, got, keys, values)


def merge(parts):
    return pl.pallas_call(
        merge_kernel,
        out_shape=jax.ShapeDtypeStruct((LINE, SLAB, HD), BF),
        in_specs=[VMEM],
        out_specs=VMEM,
        compiler_params=PARAMS,
        name="merge",
    )(parts)


def project(parts, weight):
    width = weight.shape[1]
    return pl.pallas_call(
        project_kernel,
        out_shape=jax.ShapeDtypeStruct((ROWS, width), BF),
        grid=(width // BLOCK,),
        in_specs=[
            pl.BlockSpec((LINE, SLAB, HD), lambda n: (0, 0, 0)),
            pl.BlockSpec((HD, BLOCK), lambda n: (0, n)),
        ],
        out_specs=pl.BlockSpec((ROWS, BLOCK), lambda n: (0, n)),
        scratch_shapes=[pltpu.VMEM((ROWS, HD), BF)],
        compiler_params=PARAMS,
        name="project",
    )(parts, weight)


def add(parts):
    width = parts.shape[2]
    return pl.pallas_call(
        add_kernel,
        out_shape=jax.ShapeDtypeStruct((LINE, width // 128, 128), BF),
        in_specs=[VMEM],
        out_specs=VMEM,
        scratch_shapes=[pltpu.VMEM((LINE * width // 128, 128), F32)],
        compiler_params=PARAMS,
        name="add",
    )(parts)


def lines(sections, first):
    groups = []
    for section in range(sections):
        base = section * LINE * LINE
        along_y = (section % 2 == 0) == first
        for other in range(LINE):
            step, start = (1, other * LINE) if along_y else (LINE, other)
            groups.append([base + start + step * k for k in range(LINE)])
    return groups


def exchange(value, groups):
    return lax.all_to_all(
        value, ("segment", "dev"), split_axis=0, concat_axis=0, axis_index_groups=groups, tiled=True
    )


def local(queries, page_ids, key_pages, value_pages, out_weight):
    count = lax.axis_size("segment")
    one, other = lines(count, True), lines(count, False)
    place = jnp.stack([lax.axis_index("dev"), lax.axis_index("segment") % 2]).astype(jnp.int32)
    near = exchange(prepare(queries, page_ids.reshape(KVH, SEL)), one)
    got = exchange(jnp.broadcast_to(near[None], (LINE, LINE, SLAB, HD)), other)
    partial = attend(
        place,
        got.reshape(ROWS, SLAB, HD),
        key_pages.reshape(TOKENS, HD),
        value_pages.reshape(TOKENS, HD),
    )
    joined = merge(exchange(partial.reshape(LINE, LINE, SLAB, HD), one))
    sums = project(exchange(joined, other), out_weight)
    added = add(exchange(sums.reshape(LINE, LINE, -1), other))
    parts = exchange(added, one)
    projected = jnp.sum(parts.astype(F32), axis=0).astype(BF)
    handed = lax.ppermute(projected, "segment", [(s, (s + 1) % count) for s in range(count)])
    return handed.reshape(1, -1)


def solution(mesh):
    placed = (
        P(("segment", "dev"), None),
        P(("segment", "dev"), None, None),
        P(("segment", "dev"), None, None),
        P(("segment", "dev"), None, None),
        P(("segment", "dev"), None),
    )
    return jax.shard_map(
        local, mesh=mesh, in_specs=placed, out_specs=P(("segment", "dev"), None), check_vma=False
    )
```

```python
import functools
import math

import jax
import jax.numpy as jnp
from jax import lax
from jax.experimental import pallas as pl
from jax.experimental.pallas import tpu as pltpu
from jax.sharding import PartitionSpec as P

BF = jnp.bfloat16
F32 = jnp.float32
HEADS = 64
GROUP = 16
KVH = 4
HD = 128
ROWS = 64
POOL = 16
TOKENS = 1024
SLAB = 72
PAGE = 64
SEL = 32
LINE = 8
SHARE = 4
SPAN = LINE // SHARE
OWN = ROWS // SHARE
BLOCK = 4096
CHUNK = 512
LOG2E = math.log2(math.e)
SCALE = 1.0 / math.sqrt(HD)
FAR = float(2**20)
FLOOR = -8192.0


def iota(shape, dim):
    return lax.broadcasted_iota(jnp.int32, shape, dim)


def dot(a, b):
    return lax.dot_general(a, b, (((1,), (0,)), ((), ())), preferred_element_type=F32)


def dot_nt(a, b):
    return lax.dot_general(a, b, (((1,), (1,)), ((), ())), preferred_element_type=F32)


def one_if(condition):
    return jnp.where(condition, 1.0, 0.0).astype(BF)


def prepare_kernel(q_hbm, id_hbm, out_ref, q_ref, id_ref, tmp, sems):
    q_copy = pltpu.make_async_copy(q_hbm, q_ref, sems.at[0])
    id_copy = pltpu.make_async_copy(id_hbm, id_ref, sems.at[1])
    q_copy.start()
    id_copy.start()
    q_copy.wait()
    id_copy.wait()
    for head in range(HEADS):
        tmp[head : head + 1, :] = q_ref[:, head * HD : (head + 1) * HD].astype(F32)
    ids = id_ref[...]
    tmp[HEADS:SLAB, :] = jnp.full((SLAB - HEADS, HD), -1.0, F32)
    tmp[HEADS : HEADS + KVH, 0:SEL] = (ids // POOL).astype(F32)
    tmp[HEADS + KVH : SLAB, 0:SEL] = (ids % POOL).astype(F32)
    slab = tmp[...].astype(BF)
    for copy in range(SPAN):
        out_ref[copy, :, :] = slab


def spread_kernel(x_ref, out_ref):
    for copy in range(LINE):
        out_ref[copy, :, :, :] = x_ref[...]


def attend_kernel(place_ref, q_ref, *refs):
    kv_refs = refs[:SHARE]
    out_ref, qa, point, acc, s_even, s_odd = refs[SHARE:]
    odd = place_ref[SHARE]
    ids = q_ref[:, HEADS:SLAB, :].astype(F32).reshape(OWN * 8, HD).astype(BF)
    i, j = iota((KVH * OWN, OWN * 8), 0), iota((KVH * OWN, OWN * 8), 1)
    first = (i % OWN) * 8 + i // OWN
    owner = dot(one_if(j == first), ids)
    slot = dot(one_if(j == first + KVH), ids)
    code = jnp.full((KVH * OWN, HD), -1.0, F32)
    for block in range(SHARE):
        code = jnp.where(owner == place_ref[block].astype(F32), slot + float(block * POOL), code)
    lane = iota((KVH * OWN, HD), 1).astype(F32)
    bias = jnp.full((KVH * OWN, HD), -FAR, F32)
    for j in range(SEL):
        bias = jnp.where(code[:, j : j + 1] == lane, 0.0, bias)
    bias = bias.astype(BF)
    i, j = iota((256, 256), 0), iota((256, 256), 1)
    swap = one_if((j % 16) * 16 + j // 16 == i)
    for h in range(KVH):
        for c in range(OWN // 16):
            part = q_ref[c * 16 : (c + 1) * 16, h * 16 : (h + 1) * 16, :]
            turned = dot(swap, part.reshape(256, HD)).astype(BF)
            for g in range(GROUP):
                head = h * GROUP + g
                at = jnp.where(odd == 1, head, (head % LINE) * LINE + head // LINE)
                row = pl.multiple_of(at * OWN + c * 16, 16)
                qa[pl.ds(row, 16), 0:HD] = turned[g * 16 : (g + 1) * 16, :]
                qa[pl.ds(row, 16), HD : 2 * HD] = bias[h * OWN + c * 16 : h * OWN + (c + 1) * 16, :]

    point[...] = jnp.full(point.shape, FLOOR, F32)
    acc[...] = jnp.zeros(acc.shape, F32)
    first_lane = one_if(iota((TOKENS, HD), 1) == 0)
    token_page, page_lane = iota((TOKENS, HD), 0) // PAGE, iota((TOKENS, HD), 1)

    def score(block, n):
        keys = jnp.concatenate(
            [kv_refs[block][0], one_if(page_lane == token_page + block * POOL)], axis=1
        )
        return dot_nt(qa[n * CHUNK : (n + 1) * CHUNK, :], keys)

    def finish(block, n, s_ref):
        here = slice(n * CHUNK, (n + 1) * CHUNK)
        s = s_ref[...]
        top = jnp.max(s, axis=1, keepdims=True) * SCALE
        old = point[here, :]
        new = jnp.maximum(jnp.broadcast_to(top.astype(BF).astype(F32), old.shape), old)
        point[here, :] = new
        p = jnp.exp2(s * (SCALE * LOG2E) - new[:, 0:1] * LOG2E).astype(BF)
        o = dot(p, jnp.concatenate([kv_refs[block][1], first_lane], axis=1))
        fade = jnp.exp2((old - new) * LOG2E)
        acc[here, :] = acc[here, :] * jnp.concatenate([fade, fade], axis=1) + o

    chunks = HEADS * OWN // CHUNK
    steps = [(block, n) for block in range(SHARE) for n in range(chunks)]
    slots = (s_even, s_odd)
    slots[0][...] = score(*steps[0])
    for k, step in enumerate(steps):
        if k + 1 < len(steps):
            slots[(k + 1) % 2][...] = score(*steps[k + 1])
        finish(*step, slots[k % 2])

    lane = iota((OWN, HD), 1)
    for j in range(LINE):
        stats = jnp.zeros((OWN, HD), F32)
        for i in range(LINE):
            here = slice((j * LINE + i) * OWN, (j * LINE + i + 1) * OWN)
            total = acc[here, HD : HD + 1]
            total_hi = total.astype(BF).astype(F32)
            stats = jnp.where(lane == i * 8, point[here, :], stats)
            stats = jnp.where(lane == i * 8 + 1, total_hi, stats)
            stats = jnp.where(lane == i * 8 + 2, total - total_hi, stats)
            out_ref[j, i * OWN : (i + 1) * OWN, :] = acc[here, 0:HD].astype(BF)
        out_ref[j, LINE * OWN : (LINE + 1) * OWN, :] = stats.astype(BF)


def merge_kernel(r_ref, out_ref):
    kind = iota((OWN, HD), 1) % 8
    stats_of_all = []
    for rows in range(SHARE):
        sources = [span * SHARE + rows for span in range(SPAN)]
        stats = [r_ref[src, LINE * OWN : (LINE + 1) * OWN, :].astype(F32) for src in sources]
        top = functools.reduce(jnp.maximum, stats)
        factors = [jnp.exp2((s - top) * LOG2E) for s in stats]
        total = sum(
            f * (pltpu.roll(s, HD - 1, 1) + pltpu.roll(s, HD - 2, 1))
            for f, s in zip(factors, stats)
        )
        total_hi = total.astype(BF).astype(F32)
        total_lo = pltpu.roll(total - total_hi, 2, 1)
        joint = jnp.where(kind == 1, pltpu.roll(total_hi, 1, 1), jnp.where(kind == 2, total_lo, 0.0))
        stats_of_all.append(jnp.where(kind == 0, top, joint))
        for head in range(LINE):
            acc = sum(
                f[:, head * 8 : head * 8 + 1] * r_ref[src, head * OWN : (head + 1) * OWN, :].astype(F32)
                for f, src in zip(factors, sources)
            )
            out_ref[head, rows * OWN : (rows + 1) * OWN, :] = acc.astype(BF)
    tall = jnp.concatenate(stats_of_all + [jnp.zeros((HD - ROWS, HD), F32)], axis=0).T
    for head in range(LINE):
        out_ref[head, ROWS:SLAB, :] = tall[head * 8 : (head + 1) * 8, :].astype(BF)


def project_kernel(r_ref, w_ref, out_ref, att):
    @pl.when(pl.program_id(0) == 0)
    def _():
        stats = [r_ref[src, ROWS:SLAB, :].astype(F32).T[0:ROWS, :] for src in range(LINE)]
        top = functools.reduce(jnp.maximum, [s[:, 0:1] for s in stats])
        factors = [jnp.exp2((s[:, 0:1] - top) * LOG2E) for s in stats]
        total = sum(f * (s[:, 1:2] + s[:, 2:3]) for f, s in zip(factors, stats))
        acc = sum(f * r_ref[src, 0:ROWS, :].astype(F32) for src, f in enumerate(factors))
        both = (acc / total).astype(BF)
        i, j = iota((ROWS, ROWS), 0), iota((ROWS, ROWS), 1)
        came_from = (i % SHARE) * OWN + (i // LINE) * SPAN + (i % LINE) // SHARE
        att[...] = dot(one_if(j == came_from), both).astype(BF)

    out_ref[...] = dot(att[...], w_ref[...]).astype(BF)


def add_kernel(x_ref, out_ref, tmp):
    tiles = tmp.shape[0] // LINE
    for tile in range(tiles):
        total = x_ref[0, :, tile * 128 : (tile + 1) * 128].astype(F32)
        for src in range(1, LINE):
            total += x_ref[src, :, tile * 128 : (tile + 1) * 128].astype(F32)
        tmp[pl.ds(tile, LINE, stride=tiles), :] = total
    out_ref[...] = tmp[...].reshape(LINE, tiles, 128).astype(BF)


VMEM = pl.BlockSpec(memory_space=pltpu.VMEM)
SMEM = pl.BlockSpec(memory_space=pltpu.SMEM)
PARAMS = pltpu.CompilerParams(vmem_limit_bytes=24 * 2**20)


def prepare(queries, ids):
    return pl.pallas_call(
        prepare_kernel,
        out_shape=jax.ShapeDtypeStruct((SPAN, SLAB, HD), BF),
        in_specs=[pl.BlockSpec(memory_space=pltpu.HBM)] * 2,
        out_specs=VMEM,
        scratch_shapes=[
            pltpu.VMEM(queries.shape, BF),
            pltpu.VMEM(ids.shape, jnp.int32),
            pltpu.VMEM((SLAB, HD), F32),
            pltpu.SemaphoreType.DMA((2,)),
        ],
        compiler_params=PARAMS,
        name="prepare",
    )(queries, ids)


def spread(value):
    return pl.pallas_call(
        spread_kernel,
        out_shape=jax.ShapeDtypeStruct((LINE,) + value.shape, BF),
        in_specs=[VMEM],
        out_specs=VMEM,
        compiler_params=PARAMS,
        name="spread",
    )(value)


def attend(place, got, pages):
    return pl.pallas_call(
        attend_kernel,
        out_shape=jax.ShapeDtypeStruct((LINE, (LINE + 1) * OWN, HD), BF),
        in_specs=[SMEM] + [VMEM] * (1 + SHARE),
        out_specs=VMEM,
        scratch_shapes=[
            pltpu.VMEM((HEADS * OWN, 2 * HD), BF),
            pltpu.VMEM((HEADS * OWN, HD), F32),
            pltpu.VMEM((HEADS * OWN, 2 * HD), F32),
            pltpu.VMEM((CHUNK, TOKENS), F32),
            pltpu.VMEM((CHUNK, TOKENS), F32),
        ],
        compiler_params=PARAMS,
        name="attend",
    )(place, got, *pages)


def merge(parts):
    return pl.pallas_call(
        merge_kernel,
        out_shape=jax.ShapeDtypeStruct((LINE, SLAB, HD), BF),
        in_specs=[VMEM],
        out_specs=VMEM,
        compiler_params=PARAMS,
        name="merge",
    )(parts)


def project(parts, weight):
    width = weight.shape[1]
    return pl.pallas_call(
        project_kernel,
        out_shape=jax.ShapeDtypeStruct((ROWS, width), BF),
        grid=(width // BLOCK,),
        in_specs=[
            pl.BlockSpec((LINE, SLAB, HD), lambda n: (0, 0, 0)),
            pl.BlockSpec((HD, BLOCK), lambda n: (0, n)),
        ],
        out_specs=pl.BlockSpec((ROWS, BLOCK), lambda n: (0, n)),
        scratch_shapes=[pltpu.VMEM((ROWS, HD), BF)],
        compiler_params=PARAMS,
        name="project",
    )(parts, weight)


def add(parts):
    width = parts.shape[2]
    return pl.pallas_call(
        add_kernel,
        out_shape=jax.ShapeDtypeStruct((LINE, width // 128, 128), BF),
        in_specs=[VMEM],
        out_specs=VMEM,
        scratch_shapes=[pltpu.VMEM((LINE * width // 128, 128), F32)],
        compiler_params=PARAMS,
        name="add",
    )(parts)


def lines(sections, first):
    groups = []
    for section in range(sections):
        base = section * LINE * LINE
        along_y = (section % 2 == 0) == first
        for other in range(LINE):
            step, start = (1, other * LINE) if along_y else (LINE, other)
            groups.append([base + start + step * k for k in range(LINE)])
    return groups


def exchange(value, groups):
    return lax.all_to_all(
        value, ("segment", "dev"), split_axis=0, concat_axis=0, axis_index_groups=groups, tiled=True
    )


def local(queries, page_ids, key_pages, value_pages, out_weight):
    count = lax.axis_size("segment")
    one, other = lines(count, True), lines(count, False)
    spread_over = [line[rows::SHARE] for line in one for rows in range(SHARE)]
    odd = lax.axis_index("segment") % 2
    me = lax.axis_index("dev")
    stride = jnp.where(odd == 1, LINE, 1)
    along = (me // stride) % LINE
    place = [me + ((along ^ block) - along) * stride for block in range(SHARE)]
    place = jnp.stack(place + [odd]).astype(jnp.int32)
    pages = jnp.stack([key_pages.reshape(TOKENS, HD), value_pages.reshape(TOKENS, HD)])
    shared = [pages]
    for block in range(1, SHARE):
        pairs = [(line[k], line[k ^ block]) for line in one for k in range(LINE)]
        shared.append(lax.ppermute(pages, ("segment", "dev"), pairs))
    near = exchange(prepare(queries, page_ids.reshape(KVH, SEL)), spread_over)
    got = exchange(spread(near), other)
    partial = attend(place, got.reshape(OWN, SLAB, HD), shared)
    joined = merge(exchange(partial, one))
    sums = project(exchange(joined, other), out_weight)
    added = add(exchange(sums.reshape(LINE, LINE, -1), other))
    parts = exchange(added, one)
    projected = jnp.sum(parts.astype(F32), axis=0).astype(BF)
    handed = lax.ppermute(projected, "segment", [(s, (s + 1) % count) for s in range(count)])
    return handed.reshape(1, -1)


def solution(mesh):
    placed = (
        P(("segment", "dev"), None),
        P(("segment", "dev"), None, None),
        P(("segment", "dev"), None, None),
        P(("segment", "dev"), None, None),
        P(("segment", "dev"), None),
    )
    return jax.shard_map(
        local, mesh=mesh, in_specs=placed, out_specs=P(("segment", "dev"), None), check_vma=False
    )
```

```python
import functools
import math

import jax
import jax.numpy as jnp
from jax import lax
from jax.experimental import pallas as pl
from jax.experimental.pallas import tpu as pltpu
from jax.sharding import PartitionSpec as P

BF = jnp.bfloat16
F32 = jnp.float32
HEADS = 64
GROUP = 16
KVH = 4
HD = 128
ROWS = 64
POOL = 16
TOKENS = 1024
SLAB = 72
PAGE = 64
SEL = 32
LINE = 8
SHARE = 4
SPAN = 4
PAIR = 2
OWN = ROWS // SHARE
HALF = PAIR * OWN
SMALL = HALF + 8
BLOCK = 2048
CHUNK = 512
LOG2E = math.log2(math.e)
SCALE = 1.0 / math.sqrt(HD)
FAR = float(2**20)
FLOOR = -8192.0


def iota(shape, dim):
    return lax.broadcasted_iota(jnp.int32, shape, dim)


def dot(a, b):
    return lax.dot_general(a, b, (((1,), (0,)), ((), ())), preferred_element_type=F32)


def dot_nt(a, b):
    return lax.dot_general(a, b, (((1,), (1,)), ((), ())), preferred_element_type=F32)


def one_if(condition):
    return jnp.where(condition, 1.0, 0.0).astype(BF)


def prepare_kernel(q_hbm, id_hbm, out_ref, q_ref, id_ref, tmp, sems):
    q_copy = pltpu.make_async_copy(q_hbm, q_ref, sems.at[0])
    id_copy = pltpu.make_async_copy(id_hbm, id_ref, sems.at[1])
    q_copy.start()
    id_copy.start()
    q_copy.wait()
    id_copy.wait()
    for head in range(HEADS):
        tmp[head : head + 1, :] = q_ref[:, head * HD : (head + 1) * HD].astype(F32)
    ids = id_ref[...]
    tmp[HEADS:SLAB, :] = jnp.full((SLAB - HEADS, HD), -1.0, F32)
    tmp[HEADS : HEADS + KVH, 0:SEL] = (ids // POOL).astype(F32)
    tmp[HEADS + KVH : SLAB, 0:SEL] = (ids % POOL).astype(F32)
    slab = tmp[...].astype(BF)
    for copy in range(SPAN):
        out_ref[copy, :, :] = slab


def spread_kernel(x_ref, out_ref):
    for copy in range(SPAN):
        out_ref[copy, :, :, :] = x_ref[...]


def attend_kernel(place_ref, q_ref, *refs):
    kv_refs = refs[:SHARE]
    out_ref, qa, point, acc, s_even, s_odd = refs[SHARE:]
    odd = place_ref[SHARE]
    ids = q_ref[:, HEADS:SLAB, :].astype(F32).reshape(OWN * 8, HD).astype(BF)
    i, j = iota((KVH * OWN, OWN * 8), 0), iota((KVH * OWN, OWN * 8), 1)
    first = (i % OWN) * 8 + i // OWN
    owner = dot(one_if(j == first), ids)
    slot = dot(one_if(j == first + KVH), ids)
    code = jnp.full((KVH * OWN, HD), -1.0, F32)
    for block in range(SHARE):
        code = jnp.where(owner == place_ref[block].astype(F32), slot + float(block * POOL), code)
    lane = iota((KVH * OWN, HD), 1).astype(F32)
    bias = jnp.full((KVH * OWN, HD), -FAR, F32)
    for j in range(SEL):
        bias = jnp.where(code[:, j : j + 1] == lane, 0.0, bias)
    bias = bias.astype(BF)
    i, j = iota((256, 256), 0), iota((256, 256), 1)
    swap = one_if((j % 16) * 16 + j // 16 == i)
    for h in range(KVH):
        for c in range(OWN // 16):
            part = q_ref[c * 16 : (c + 1) * 16, h * 16 : (h + 1) * 16, :]
            turned = dot(swap, part.reshape(256, HD)).astype(BF)
            for g in range(GROUP):
                head = h * GROUP + g
                at = jnp.where(odd == 1, head, (head % LINE) * LINE + head // LINE)
                row = pl.multiple_of(at * OWN + c * 16, 16)
                qa[pl.ds(row, 16), 0:HD] = turned[g * 16 : (g + 1) * 16, :]
                qa[pl.ds(row, 16), HD : 2 * HD] = bias[h * OWN + c * 16 : h * OWN + (c + 1) * 16, :]

    point[...] = jnp.full(point.shape, FLOOR, F32)
    acc[...] = jnp.zeros(acc.shape, F32)
    first_lane = one_if(iota((TOKENS, HD), 1) == 0)
    token_page, page_lane = iota((TOKENS, HD), 0) // PAGE, iota((TOKENS, HD), 1)

    def score(block, n):
        keys = jnp.concatenate(
            [kv_refs[block][0], one_if(page_lane == token_page + block * POOL)], axis=1
        )
        return dot_nt(qa[n * CHUNK : (n + 1) * CHUNK, :], keys)

    def finish(block, n, s_ref):
        here = slice(n * CHUNK, (n + 1) * CHUNK)
        s = s_ref[...]
        top = jnp.max(s, axis=1, keepdims=True) * SCALE
        old = point[here, :]
        new = jnp.maximum(jnp.broadcast_to(top.astype(BF).astype(F32), old.shape), old)
        point[here, :] = new
        p = jnp.exp2(s * (SCALE * LOG2E) - new[:, 0:1] * LOG2E).astype(BF)
        o = dot(p, jnp.concatenate([kv_refs[block][1], first_lane], axis=1))
        fade = jnp.exp2((old - new) * LOG2E)
        acc[here, :] = acc[here, :] * jnp.concatenate([fade, fade], axis=1) + o

    chunks = HEADS * OWN // CHUNK
    steps = [(block, n) for block in range(SHARE) for n in range(chunks)]
    slots = (s_even, s_odd)
    slots[0][...] = score(*steps[0])
    for k, step in enumerate(steps):
        if k + 1 < len(steps):
            slots[(k + 1) % 2][...] = score(*steps[k + 1])
        finish(*step, slots[k % 2])

    lane = iota((OWN, HD), 1)
    for j in range(LINE):
        stats = jnp.zeros((OWN, HD), F32)
        for i in range(LINE):
            here = slice((j * LINE + i) * OWN, (j * LINE + i + 1) * OWN)
            total = acc[here, HD : HD + 1]
            total_hi = total.astype(BF).astype(F32)
            stats = jnp.where(lane == i * 8, point[here, :], stats)
            stats = jnp.where(lane == i * 8 + 1, total_hi, stats)
            stats = jnp.where(lane == i * 8 + 2, total - total_hi, stats)
            out_ref[j, i * OWN : (i + 1) * OWN, :] = acc[here, 0:HD].astype(BF)
        out_ref[j, LINE * OWN : (LINE + 1) * OWN, :] = stats.astype(BF)


def merge_kernel(r_ref, out_ref):
    kind = iota((OWN, HD), 1) % 8
    stats_of_all = []
    for rows in range(PAIR):
        sources = range(rows, LINE, PAIR)
        stats = [r_ref[src, LINE * OWN : (LINE + 1) * OWN, :].astype(F32) for src in sources]
        top = functools.reduce(jnp.maximum, stats)
        factors = [jnp.exp2((s - top) * LOG2E) for s in stats]
        total = sum(
            f * (pltpu.roll(s, HD - 1, 1) + pltpu.roll(s, HD - 2, 1))
            for f, s in zip(factors, stats)
        )
        total_hi = total.astype(BF).astype(F32)
        total_lo = pltpu.roll(total - total_hi, 2, 1)
        joint = jnp.where(kind == 1, pltpu.roll(total_hi, 1, 1), jnp.where(kind == 2, total_lo, 0.0))
        stats_of_all.append(jnp.where(kind == 0, top, joint))
        for head in range(LINE):
            acc = sum(
                f[:, head * 8 : head * 8 + 1] * r_ref[src, head * OWN : (head + 1) * OWN, :].astype(F32)
                for f, src in zip(factors, sources)
            ).astype(BF)
            out_ref[head, 0, rows * OWN : (rows + 1) * OWN, :] = acc
            out_ref[head ^ 1, 1, rows * OWN : (rows + 1) * OWN, :] = acc
    tall = jnp.concatenate(stats_of_all + [jnp.zeros((HD - HALF, HD), F32)], axis=0).T
    for head in range(LINE):
        stats = tall[head * 8 : (head + 1) * 8, :].astype(BF)
        out_ref[head, 0, HALF:SMALL, :] = stats
        out_ref[head ^ 1, 1, HALF:SMALL, :] = stats


def project_kernel(side_ref, r_ref, mine_ref, theirs_ref, out_ref, att):
    @pl.when(pl.program_id(0) == 0)
    def _():
        heads = []
        for head in range(PAIR):
            halves = []
            for rows in range(PAIR):
                sources = range(rows, LINE, PAIR)
                stats = [r_ref[src, head, HALF:SMALL, :].astype(F32).T[0:HALF, :] for src in sources]
                top = functools.reduce(jnp.maximum, [s[:, 0:1] for s in stats])
                factors = [jnp.exp2((s[:, 0:1] - top) * LOG2E) for s in stats]
                total = sum(f * (s[:, 1:2] + s[:, 2:3]) for f, s in zip(factors, stats))
                acc = sum(
                    f * r_ref[src, head, 0:HALF, :].astype(F32) for src, f in zip(sources, factors)
                )
                halves.append((acc / total).astype(BF))
            heads.append(jnp.concatenate(halves, axis=0))
        both = jnp.concatenate(heads, axis=1)
        i, j = iota((ROWS, ROWS), 0), iota((ROWS, ROWS), 1)
        b, u = i // LINE, i % LINE
        came_from = (b % PAIR) * HALF + (u % PAIR) * OWN + (b // PAIR) * SPAN + u // PAIR
        att[...] = dot(one_if(j == came_from), both).astype(BF)

    weight = jnp.concatenate([mine_ref[...], theirs_ref[...]], axis=0)
    out_ref[...] = dot(att[...], weight).astype(BF)


def add_kernel(x_ref, out_ref, tmp):
    tiles = tmp.shape[0] // LINE
    half = tiles // PAIR
    for tile in range(tiles):
        lanes = slice(tile % half * 128, (tile % half + 1) * 128)
        total = sum(x_ref[src, :, lanes].astype(F32) for src in range(tile // half, LINE, PAIR))
        tmp[pl.ds(tile, LINE, stride=tiles), :] = total
    out_ref[...] = tmp[...].reshape(LINE, tiles, 128).astype(BF)


VMEM = pl.BlockSpec(memory_space=pltpu.VMEM)
SMEM = pl.BlockSpec(memory_space=pltpu.SMEM)
PARAMS = pltpu.CompilerParams(vmem_limit_bytes=24 * 2**20)


def prepare(queries, ids):
    return pl.pallas_call(
        prepare_kernel,
        out_shape=jax.ShapeDtypeStruct((SPAN, SLAB, HD), BF),
        in_specs=[pl.BlockSpec(memory_space=pltpu.HBM)] * 2,
        out_specs=VMEM,
        scratch_shapes=[
            pltpu.VMEM(queries.shape, BF),
            pltpu.VMEM(ids.shape, jnp.int32),
            pltpu.VMEM((SLAB, HD), F32),
            pltpu.SemaphoreType.DMA((2,)),
        ],
        compiler_params=PARAMS,
        name="prepare",
    )(queries, ids)


def spread(value):
    return pl.pallas_call(
        spread_kernel,
        out_shape=jax.ShapeDtypeStruct((SPAN,) + value.shape, BF),
        in_specs=[VMEM],
        out_specs=VMEM,
        compiler_params=PARAMS,
        name="spread",
    )(value)


def attend(place, got, pages):
    return pl.pallas_call(
        attend_kernel,
        out_shape=jax.ShapeDtypeStruct((LINE, (LINE + 1) * OWN, HD), BF),
        in_specs=[SMEM] + [VMEM] * (1 + SHARE),
        out_specs=VMEM,
        scratch_shapes=[
            pltpu.VMEM((HEADS * OWN, 2 * HD), BF),
            pltpu.VMEM((HEADS * OWN, HD), F32),
            pltpu.VMEM((HEADS * OWN, 2 * HD), F32),
            pltpu.VMEM((CHUNK, TOKENS), F32),
            pltpu.VMEM((CHUNK, TOKENS), F32),
        ],
        compiler_params=PARAMS,
        name="attend",
    )(place, got, *pages)


def merge(parts):
    return pl.pallas_call(
        merge_kernel,
        out_shape=jax.ShapeDtypeStruct((LINE, PAIR, SMALL, HD), BF),
        in_specs=[VMEM],
        out_specs=VMEM,
        compiler_params=PARAMS,
        name="merge",
    )(parts)


def project(side, parts, mine, theirs):
    width = theirs.shape[1]
    steps = width // BLOCK
    return pl.pallas_call(
        project_kernel,
        out_shape=jax.ShapeDtypeStruct((ROWS, width), BF),
        grid_spec=pltpu.PrefetchScalarGridSpec(
            num_scalar_prefetch=1,
            grid=(steps,),
            in_specs=[
                pl.BlockSpec(parts.shape, lambda n, side: (0, 0, 0, 0)),
                pl.BlockSpec((HD, BLOCK), lambda n, side: (0, n + side[0] * steps)),
                pl.BlockSpec((HD, BLOCK), lambda n, side: (0, n)),
            ],
            out_specs=pl.BlockSpec((ROWS, BLOCK), lambda n, side: (0, n)),
            scratch_shapes=[pltpu.VMEM((ROWS, PAIR * HD), BF)],
        ),
        compiler_params=PARAMS,
        name="project",
    )(side, parts, mine, theirs)


def add(parts):
    width = parts.shape[2] * PAIR
    return pl.pallas_call(
        add_kernel,
        out_shape=jax.ShapeDtypeStruct((LINE, width // 128, 128), BF),
        in_specs=[VMEM],
        out_specs=VMEM,
        scratch_shapes=[pltpu.VMEM((LINE * width // 128, 128), F32)],
        compiler_params=PARAMS,
        name="add",
    )(parts)


def lines(sections, first):
    groups = []
    for section in range(sections):
        base = section * LINE * LINE
        along_y = (section % 2 == 0) == first
        for other in range(LINE):
            step, start = (1, other * LINE) if along_y else (LINE, other)
            groups.append([base + start + step * k for k in range(LINE)])
    return groups


def exchange(value, groups):
    return lax.all_to_all(
        value, ("segment", "dev"), split_axis=0, concat_axis=0, axis_index_groups=groups, tiled=True
    )


def in_hbm(value):
    return pltpu.with_memory_space_constraint(value, pltpu.HBM)


def neighbours(groups):
    return [(line[k], line[k ^ 1]) for line in groups for k in range(LINE)]


def local(queries, page_ids, key_pages, value_pages, out_weight):
    count = lax.axis_size("segment")
    both = ("segment", "dev")
    one, other = lines(count, True), lines(count, False)
    one_rows = [line[rows::PAIR] for line in one for rows in range(PAIR)]
    other_rows = [line[rows::PAIR] for line in other for rows in range(PAIR)]
    odd = lax.axis_index("segment") % 2
    me = lax.axis_index("dev")
    u = jnp.where(odd == 1, me // LINE, me % LINE)
    b = jnp.where(odd == 1, me % LINE, me // LINE)
    place = []
    for block in range(SHARE):
        block_u, block_b = u ^ (block % 2), b ^ (block // 2)
        place.append(jnp.where(odd == 1, block_u * LINE + block_b, block_b * LINE + block_u))
    place = jnp.stack(place + [odd]).astype(jnp.int32)

    near = exchange(prepare(in_hbm(queries), in_hbm(page_ids.reshape(KVH, SEL))), one_rows)
    pages = jnp.stack([key_pages.reshape(TOKENS, HD), value_pages.reshape(TOKENS, HD)])
    pages_u = lax.ppermute(pages, both, neighbours(one))
    pages_b = lax.ppermute(pages, both, neighbours(other))
    near, pages_u, pages_b = lax.optimization_barrier((near, pages_u, pages_b))
    pages_ub = lax.ppermute(pages_u, both, neighbours(other))
    got = exchange(spread(near), other_rows)

    side = b % PAIR
    width = out_weight.shape[1] // PAIR
    weight, got, pages_ub = lax.optimization_barrier((out_weight, got, pages_ub))
    given = lax.dynamic_slice_in_dim(weight, (1 - side) * width, width, axis=1)
    theirs = lax.ppermute(given, both, neighbours(other))

    partial = attend(place, got.reshape(OWN, SLAB, HD), [pages, pages_u, pages_b, pages_ub])
    joined = merge(exchange(partial, one))
    gathered = exchange(joined, other)
    sums = project(side.astype(jnp.int32).reshape(1), gathered, in_hbm(out_weight), theirs)
    added = add(exchange(sums.reshape(LINE, LINE, -1), other))
    parts = exchange(added, one)
    projected = jnp.sum(parts.astype(F32), axis=0).astype(BF)
    handed = lax.ppermute(projected, "segment", [(s, (s + 1) % count) for s in range(count)])
    return handed.reshape(1, -1)


def solution(mesh):
    placed = (
        P(("segment", "dev"), None),
        P(("segment", "dev"), None, None),
        P(("segment", "dev"), None, None),
        P(("segment", "dev"), None, None),
        P(("segment", "dev"), None),
    )
    return jax.shard_map(
        local, mesh=mesh, in_specs=placed, out_specs=P(("segment", "dev"), None), check_vma=False
    )
```

```python
import functools
import math

import jax
import jax.numpy as jnp
from jax import lax
from jax.experimental import pallas as pl
from jax.experimental.pallas import tpu as pltpu
from jax.sharding import PartitionSpec as P

BF = jnp.bfloat16
F32 = jnp.float32
HEADS = 64
GROUP = 16
KVH = 4
HD = 128
ROWS = 64
POOL = 16
TOKENS = 1024
SLAB = 72
PAGE = 64
SEL = 32
LINE = 8
SHARE = 4
SPAN = 4
PAIR = 2
OWN = ROWS // SHARE
HALF = PAIR * OWN
SMALL = HALF + 8
BLOCK = 2048
CHUNK = 512
LOG2E = math.log2(math.e)
SCALE = 1.0 / math.sqrt(HD)
FAR = float(2**20)
FLOOR = -8192.0


def iota(shape, dim):
    return lax.broadcasted_iota(jnp.int32, shape, dim)


def dot(a, b):
    return lax.dot_general(a, b, (((1,), (0,)), ((), ())), preferred_element_type=F32)


def dot_nt(a, b):
    return lax.dot_general(a, b, (((1,), (1,)), ((), ())), preferred_element_type=F32)


def one_if(condition):
    return jnp.where(condition, 1.0, 0.0).astype(BF)


def prepare_kernel(q_hbm, id_hbm, k_hbm, v_hbm, out_ref, pages_hbm, q_ref, id_ref, tmp, sems):
    copies = [
        pltpu.make_async_copy(q_hbm, q_ref, sems.at[0]),
        pltpu.make_async_copy(id_hbm, id_ref, sems.at[1]),
        pltpu.make_async_copy(k_hbm, pages_hbm.at[0], sems.at[2]),
        pltpu.make_async_copy(v_hbm, pages_hbm.at[1], sems.at[3]),
    ]
    for copy in copies:
        copy.start()
    copies[0].wait()
    copies[1].wait()
    for head in range(HEADS):
        tmp[head : head + 1, :] = q_ref[:, head * HD : (head + 1) * HD].astype(F32)
    ids = id_ref[...]
    tmp[HEADS:SLAB, :] = jnp.full((SLAB - HEADS, HD), -1.0, F32)
    tmp[HEADS : HEADS + KVH, 0:SEL] = (ids // POOL).astype(F32)
    tmp[HEADS + KVH : SLAB, 0:SEL] = (ids % POOL).astype(F32)
    slab = tmp[...].astype(BF)
    for copy in range(SPAN):
        out_ref[copy, :, :] = slab
    copies[2].wait()
    copies[3].wait()


def halves_kernel(side_ref, w_hbm, mine_ref, given_ref, sems):
    width = mine_ref.shape[1]
    side = side_ref[0]
    mine = pl.ds(pl.multiple_of(side * width, width), width)
    given = pl.ds(pl.multiple_of((1 - side) * width, width), width)
    copies = [
        pltpu.make_async_copy(w_hbm.at[:, given], given_ref, sems.at[0]),
        pltpu.make_async_copy(w_hbm.at[:, mine], mine_ref, sems.at[1]),
    ]
    for copy in copies:
        copy.start()
    for copy in copies:
        copy.wait()


def spread_kernel(x_ref, out_ref):
    for copy in range(SPAN):
        out_ref[copy, :, :, :] = x_ref[...]


def attend_kernel(place_ref, q_ref, *refs):
    kv_hbms = refs[:SHARE]
    out_ref, kv_refs, sems, qa, point, acc, s_even, s_odd = refs[SHARE:]
    copies = [
        pltpu.make_async_copy(kv_hbms[block], kv_refs.at[block], sems.at[block])
        for block in range(SHARE)
    ]
    for copy in copies:
        copy.start()
    odd = place_ref[SHARE]
    ids = q_ref[:, HEADS:SLAB, :].astype(F32).reshape(OWN * 8, HD).astype(BF)
    i, j = iota((KVH * OWN, OWN * 8), 0), iota((KVH * OWN, OWN * 8), 1)
    first = (i % OWN) * 8 + i // OWN
    owner = dot(one_if(j == first), ids)
    slot = dot(one_if(j == first + KVH), ids)
    code = jnp.full((KVH * OWN, HD), -1.0, F32)
    for block in range(SHARE):
        code = jnp.where(owner == place_ref[block].astype(F32), slot + float(block * POOL), code)
    lane = iota((KVH * OWN, HD), 1).astype(F32)
    bias = jnp.full((KVH * OWN, HD), -FAR, F32)
    for j in range(SEL):
        bias = jnp.where(code[:, j : j + 1] == lane, 0.0, bias)
    bias = bias.astype(BF)
    i, j = iota((256, 256), 0), iota((256, 256), 1)
    swap = one_if((j % 16) * 16 + j // 16 == i)
    for h in range(KVH):
        for c in range(OWN // 16):
            part = q_ref[c * 16 : (c + 1) * 16, h * 16 : (h + 1) * 16, :]
            turned = dot(swap, part.reshape(256, HD)).astype(BF)
            for g in range(GROUP):
                head = h * GROUP + g
                at = jnp.where(odd == 1, head, (head % LINE) * LINE + head // LINE)
                row = pl.multiple_of(at * OWN + c * 16, 16)
                qa[pl.ds(row, 16), 0:HD] = turned[g * 16 : (g + 1) * 16, :]
                qa[pl.ds(row, 16), HD : 2 * HD] = bias[h * OWN + c * 16 : h * OWN + (c + 1) * 16, :]

    point[...] = jnp.full(point.shape, FLOOR, F32)
    acc[...] = jnp.zeros(acc.shape, F32)
    first_lane = one_if(iota((TOKENS, HD), 1) == 0)
    token_page, page_lane = iota((TOKENS, HD), 0) // PAGE, iota((TOKENS, HD), 1)

    def score(block, n):
        keys = jnp.concatenate(
            [kv_refs[block, 0], one_if(page_lane == token_page + block * POOL)], axis=1
        )
        return dot_nt(qa[n * CHUNK : (n + 1) * CHUNK, :], keys)

    def finish(block, n, s_ref):
        here = slice(n * CHUNK, (n + 1) * CHUNK)
        s = s_ref[...]
        top = jnp.max(s, axis=1, keepdims=True) * SCALE
        old = point[here, :]
        new = jnp.maximum(jnp.broadcast_to(top.astype(BF).astype(F32), old.shape), old)
        point[here, :] = new
        p = jnp.exp2(s * (SCALE * LOG2E) - new[:, 0:1] * LOG2E).astype(BF)
        o = dot(p, jnp.concatenate([kv_refs[block, 1], first_lane], axis=1))
        fade = jnp.exp2((old - new) * LOG2E)
        acc[here, :] = acc[here, :] * jnp.concatenate([fade, fade], axis=1) + o

    for copy in copies:
        copy.wait()
    chunks = HEADS * OWN // CHUNK
    steps = [(block, n) for block in range(SHARE) for n in range(chunks)]
    slots = (s_even, s_odd)
    slots[0][...] = score(*steps[0])
    for k, step in enumerate(steps):
        if k + 1 < len(steps):
            slots[(k + 1) % 2][...] = score(*steps[k + 1])
        finish(*step, slots[k % 2])

    lane = iota((OWN, HD), 1)
    for j in range(LINE):
        stats = jnp.zeros((OWN, HD), F32)
        for i in range(LINE):
            here = slice((j * LINE + i) * OWN, (j * LINE + i + 1) * OWN)
            total = acc[here, HD : HD + 1]
            total_hi = total.astype(BF).astype(F32)
            stats = jnp.where(lane == i * 8, point[here, :], stats)
            stats = jnp.where(lane == i * 8 + 1, total_hi, stats)
            stats = jnp.where(lane == i * 8 + 2, total - total_hi, stats)
            out_ref[j, i * OWN : (i + 1) * OWN, :] = acc[here, 0:HD].astype(BF)
        out_ref[j, LINE * OWN : (LINE + 1) * OWN, :] = stats.astype(BF)


def merge_kernel(r_ref, out_ref):
    kind = iota((OWN, HD), 1) % 8
    stats_of_all = []
    for rows in range(PAIR):
        sources = range(rows, LINE, PAIR)
        stats = [r_ref[src, LINE * OWN : (LINE + 1) * OWN, :].astype(F32) for src in sources]
        top = functools.reduce(jnp.maximum, stats)
        factors = [jnp.exp2((s - top) * LOG2E) for s in stats]
        total = sum(
            f * (pltpu.roll(s, HD - 1, 1) + pltpu.roll(s, HD - 2, 1))
            for f, s in zip(factors, stats)
        )
        total_hi = total.astype(BF).astype(F32)
        total_lo = pltpu.roll(total - total_hi, 2, 1)
        joint = jnp.where(kind == 1, pltpu.roll(total_hi, 1, 1), jnp.where(kind == 2, total_lo, 0.0))
        stats_of_all.append(jnp.where(kind == 0, top, joint))
        for head in range(LINE):
            acc = sum(
                f[:, head * 8 : head * 8 + 1] * r_ref[src, head * OWN : (head + 1) * OWN, :].astype(F32)
                for f, src in zip(factors, sources)
            ).astype(BF)
            out_ref[head, 0, rows * OWN : (rows + 1) * OWN, :] = acc
            out_ref[head ^ 1, 1, rows * OWN : (rows + 1) * OWN, :] = acc
    tall = jnp.concatenate(stats_of_all + [jnp.zeros((HD - HALF, HD), F32)], axis=0).T
    for head in range(LINE):
        stats = tall[head * 8 : (head + 1) * 8, :].astype(BF)
        out_ref[head, 0, HALF:SMALL, :] = stats
        out_ref[head ^ 1, 1, HALF:SMALL, :] = stats


def project_kernel(r_ref, mine_ref, theirs_ref, out_ref, att):
    heads = []
    for head in range(PAIR):
        halves = []
        for rows in range(PAIR):
            sources = range(rows, LINE, PAIR)
            stats = [r_ref[src, head, HALF:SMALL, :].astype(F32).T[0:HALF, :] for src in sources]
            top = functools.reduce(jnp.maximum, [s[:, 0:1] for s in stats])
            factors = [jnp.exp2((s[:, 0:1] - top) * LOG2E) for s in stats]
            total = sum(f * (s[:, 1:2] + s[:, 2:3]) for f, s in zip(factors, stats))
            acc = sum(
                f * r_ref[src, head, 0:HALF, :].astype(F32) for src, f in zip(sources, factors)
            )
            halves.append((acc / total).astype(BF))
        heads.append(jnp.concatenate(halves, axis=0))
    both = jnp.concatenate(heads, axis=1)
    i, j = iota((ROWS, ROWS), 0), iota((ROWS, ROWS), 1)
    b, u = i // LINE, i % LINE
    came_from = (b % PAIR) * HALF + (u % PAIR) * OWN + (b // PAIR) * SPAN + u // PAIR
    att[...] = dot(one_if(j == came_from), both).astype(BF)

    for n in range(out_ref.shape[1] // BLOCK):
        lanes = slice(n * BLOCK, (n + 1) * BLOCK)
        weight = jnp.concatenate([mine_ref[:, lanes], theirs_ref[:, lanes]], axis=0)
        out_ref[:, lanes] = dot(att[...], weight).astype(BF)


def add_kernel(x_ref, out_ref, tmp):
    tiles = tmp.shape[0] // LINE
    half = tiles // PAIR
    for tile in range(tiles):
        lanes = slice(tile % half * 128, (tile % half + 1) * 128)
        total = sum(x_ref[src, :, lanes].astype(F32) for src in range(tile // half, LINE, PAIR))
        tmp[pl.ds(tile, LINE, stride=tiles), :] = total
    out_ref[...] = tmp[...].reshape(LINE, tiles, 128).astype(BF)


VMEM = pl.BlockSpec(memory_space=pltpu.VMEM)
ANYWHERE = pl.BlockSpec(memory_space=pl.ANY)
SMEM = pl.BlockSpec(memory_space=pltpu.SMEM)
PARAMS = pltpu.CompilerParams(vmem_limit_bytes=24 * 2**20)


def in_hbm(value):
    return pltpu.with_memory_space_constraint(value, pltpu.HBM)


def prepare(queries, ids, keys, values):
    return pl.pallas_call(
        prepare_kernel,
        out_shape=(
            jax.ShapeDtypeStruct((SPAN, SLAB, HD), BF),
            pltpu.HBM((2, TOKENS, HD), BF),
        ),
        in_specs=[ANYWHERE] * 4,
        out_specs=(VMEM, ANYWHERE),
        scratch_shapes=[
            pltpu.VMEM(queries.shape, BF),
            pltpu.VMEM(ids.shape, jnp.int32),
            pltpu.VMEM((SLAB, HD), F32),
            pltpu.SemaphoreType.DMA((4,)),
        ],
        compiler_params=PARAMS,
        name="prepare",
    )(*[in_hbm(value) for value in (queries, ids, keys, values)])


def halves(side, weight):
    half = jax.ShapeDtypeStruct((HD, weight.shape[1] // PAIR), BF)
    return pl.pallas_call(
        halves_kernel,
        out_shape=(half, half),
        in_specs=[SMEM, ANYWHERE],
        out_specs=(VMEM, VMEM),
        scratch_shapes=[pltpu.SemaphoreType.DMA((2,))],
        compiler_params=PARAMS,
        name="halves",
    )(side, in_hbm(weight))


def spread(value):
    return pl.pallas_call(
        spread_kernel,
        out_shape=jax.ShapeDtypeStruct((SPAN,) + value.shape, BF),
        in_specs=[VMEM],
        out_specs=VMEM,
        compiler_params=PARAMS,
        name="spread",
    )(value)


def attend(place, got, pages):
    return pl.pallas_call(
        attend_kernel,
        out_shape=jax.ShapeDtypeStruct((LINE, (LINE + 1) * OWN, HD), BF),
        in_specs=[SMEM, VMEM] + [ANYWHERE] * SHARE,
        out_specs=VMEM,
        scratch_shapes=[
            pltpu.VMEM((SHARE, 2, TOKENS, HD), BF),
            pltpu.SemaphoreType.DMA((SHARE,)),
            pltpu.VMEM((HEADS * OWN, 2 * HD), BF),
            pltpu.VMEM((HEADS * OWN, HD), F32),
            pltpu.VMEM((HEADS * OWN, 2 * HD), F32),
            pltpu.VMEM((CHUNK, TOKENS), F32),
            pltpu.VMEM((CHUNK, TOKENS), F32),
        ],
        compiler_params=PARAMS,
        name="attend",
    )(place, got, *[in_hbm(block) for block in pages])


def merge(parts):
    return pl.pallas_call(
        merge_kernel,
        out_shape=jax.ShapeDtypeStruct((LINE, PAIR, SMALL, HD), BF),
        in_specs=[VMEM],
        out_specs=VMEM,
        compiler_params=PARAMS,
        name="merge",
    )(parts)


def project(parts, mine, theirs):
    width = theirs.shape[1]
    return pl.pallas_call(
        project_kernel,
        out_shape=jax.ShapeDtypeStruct((ROWS, width), BF),
        in_specs=[VMEM] * 3,
        out_specs=VMEM,
        scratch_shapes=[pltpu.VMEM((ROWS, PAIR * HD), BF)],
        compiler_params=PARAMS,
        name="project",
    )(parts, mine, theirs)


def add(parts):
    width = parts.shape[2] * PAIR
    return pl.pallas_call(
        add_kernel,
        out_shape=jax.ShapeDtypeStruct((LINE, width // 128, 128), BF),
        in_specs=[VMEM],
        out_specs=VMEM,
        scratch_shapes=[pltpu.VMEM((LINE * width // 128, 128), F32)],
        compiler_params=PARAMS,
        name="add",
    )(parts)


def lines(sections, first):
    groups = []
    for section in range(sections):
        base = section * LINE * LINE
        along_y = (section % 2 == 0) == first
        for other in range(LINE):
            step, start = (1, other * LINE) if along_y else (LINE, other)
            groups.append([base + start + step * k for k in range(LINE)])
    return groups


def exchange(value, groups):
    return lax.all_to_all(
        value, ("segment", "dev"), split_axis=0, concat_axis=0, axis_index_groups=groups, tiled=True
    )


def neighbours(groups):
    return [(line[k], line[k ^ 1]) for line in groups for k in range(LINE)]


def local(queries, page_ids, key_pages, value_pages, out_weight):
    count = lax.axis_size("segment")
    both = ("segment", "dev")
    one, other = lines(count, True), lines(count, False)
    one_rows = [line[rows::PAIR] for line in one for rows in range(PAIR)]
    other_rows = [line[rows::PAIR] for line in other for rows in range(PAIR)]
    odd = lax.axis_index("segment") % 2
    me = lax.axis_index("dev")
    u = jnp.where(odd == 1, me // LINE, me % LINE)
    b = jnp.where(odd == 1, me % LINE, me // LINE)
    place = []
    for block in range(SHARE):
        block_u, block_b = u ^ (block % 2), b ^ (block // 2)
        place.append(jnp.where(odd == 1, block_u * LINE + block_b, block_b * LINE + block_u))
    place = jnp.stack(place + [odd]).astype(jnp.int32)

    payload, pages = prepare(
        queries,
        page_ids.reshape(KVH, SEL),
        key_pages.reshape(TOKENS, HD),
        value_pages.reshape(TOKENS, HD),
    )
    mine, given = halves((b % PAIR).astype(jnp.int32).reshape(1), out_weight)
    near = exchange(payload, one_rows)
    pages_u = lax.ppermute(pages, both, neighbours(one))
    pages_b = lax.ppermute(pages, both, neighbours(other))
    near, came_u, _, given = lax.optimization_barrier((near, pages_u, pages_b, given))
    pages_ub = lax.ppermute(came_u, both, neighbours(other))
    got = exchange(spread(near), other_rows)
    given, got, _ = lax.optimization_barrier((given, got, pages_ub))
    theirs = lax.ppermute(given, both, neighbours(other))

    partial = attend(place, got.reshape(OWN, SLAB, HD), [pages, pages_u, pages_b, pages_ub])
    joined = merge(exchange(partial, one))
    gathered = exchange(joined, other)
    sums = project(gathered, mine, theirs)
    added = add(exchange(sums.reshape(LINE, LINE, -1), other))
    parts = exchange(added, one)
    projected = jnp.sum(parts.astype(F32), axis=0).astype(BF)
    handed = lax.ppermute(projected, "segment", [(s, (s + 1) % count) for s in range(count)])
    return handed.reshape(1, -1)


def solution(mesh):
    placed = (
        P(("segment", "dev"), None),
        P(("segment", "dev"), None, None),
        P(("segment", "dev"), None, None),
        P(("segment", "dev"), None, None),
        P(("segment", "dev"), None),
    )
    return jax.shard_map(
        local, mesh=mesh, in_specs=placed, out_specs=P(("segment", "dev"), None), check_vma=False
    )
```

```python
import functools
import math

import jax
import jax.numpy as jnp
from jax import lax
from jax.experimental import pallas as pl
from jax.experimental.pallas import tpu as pltpu
from jax.sharding import PartitionSpec as P

BF = jnp.bfloat16
F32 = jnp.float32
HEADS = 64
GROUP = 16
KVH = 4
HD = 128
ROWS = 64
POOL = 16
TOKENS = 1024
SLAB = 72
PAGE = 64
SEL = 32
LINE = 8
SHARE = 4
SPAN = 4
PAIR = 2
OWN = ROWS // SHARE
HALF = PAIR * OWN
SMALL = HALF + 8
BLOCK = 2048
CHUNK = 512
LOG2E = math.log2(math.e)
SCALE = 1.0 / math.sqrt(HD)
FAR = float(2**20)
FLOOR = -8192.0


def iota(shape, dim):
    return lax.broadcasted_iota(jnp.int32, shape, dim)


def dot(a, b):
    return lax.dot_general(a, b, (((1,), (0,)), ((), ())), preferred_element_type=F32)


def dot_nt(a, b):
    return lax.dot_general(a, b, (((1,), (1,)), ((), ())), preferred_element_type=F32)


def one_if(condition):
    return jnp.where(condition, 1.0, 0.0).astype(BF)


def prepare_kernel(q_hbm, id_hbm, k_hbm, v_hbm, out_ref, pages_ref, q_ref, id_ref, tmp, sems):
    copies = [
        pltpu.make_async_copy(q_hbm, q_ref, sems.at[0]),
        pltpu.make_async_copy(id_hbm, id_ref, sems.at[1]),
        pltpu.make_async_copy(k_hbm, pages_ref.at[0], sems.at[2]),
        pltpu.make_async_copy(v_hbm, pages_ref.at[1], sems.at[3]),
    ]
    for copy in copies:
        copy.start()
    copies[0].wait()
    copies[1].wait()
    for head in range(HEADS):
        tmp[head : head + 1, :] = q_ref[:, head * HD : (head + 1) * HD].astype(F32)
    ids = id_ref[...]
    tmp[HEADS:SLAB, :] = jnp.full((SLAB - HEADS, HD), -1.0, F32)
    tmp[HEADS : HEADS + KVH, 0:SEL] = (ids // POOL).astype(F32)
    tmp[HEADS + KVH : SLAB, 0:SEL] = (ids % POOL).astype(F32)
    slab = tmp[...].astype(BF)
    for copy in range(SPAN):
        out_ref[copy, :, :] = slab
    copies[2].wait()
    copies[3].wait()


def halves_kernel(side_ref, w_hbm, mine_ref, given_ref, sems):
    width = mine_ref.shape[1]
    side = side_ref[0]
    mine = pl.ds(pl.multiple_of(side * width, width), width)
    given = pl.ds(pl.multiple_of((1 - side) * width, width), width)
    copies = [
        pltpu.make_async_copy(w_hbm.at[:, given], given_ref, sems.at[0]),
        pltpu.make_async_copy(w_hbm.at[:, mine], mine_ref, sems.at[1]),
    ]
    for copy in copies:
        copy.start()
    for copy in copies:
        copy.wait()


def spread_kernel(x_ref, out_ref):
    for copy in range(SPAN):
        out_ref[copy, :, :, :] = x_ref[...]


def attend_kernel(place_ref, q_ref, *refs):
    kv_hbms = refs[:SHARE]
    out_ref, kv_refs, sems, qa, point, acc, s_even, s_odd = refs[SHARE:]
    copies = [
        pltpu.make_async_copy(kv_hbms[block], kv_refs.at[block], sems.at[block])
        for block in range(SHARE)
    ]
    for copy in copies:
        copy.start()
    odd = place_ref[SHARE]
    ids = q_ref[:, HEADS:SLAB, :].astype(F32).reshape(OWN * 8, HD).astype(BF)
    i, j = iota((KVH * OWN, OWN * 8), 0), iota((KVH * OWN, OWN * 8), 1)
    first = (i % OWN) * 8 + i // OWN
    owner = dot(one_if(j == first), ids)
    slot = dot(one_if(j == first + KVH), ids)
    code = jnp.full((KVH * OWN, HD), -1.0, F32)
    for block in range(SHARE):
        code = jnp.where(owner == place_ref[block].astype(F32), slot + float(block * POOL), code)
    lane = iota((KVH * OWN, HD), 1).astype(F32)
    bias = jnp.full((KVH * OWN, HD), -FAR, F32)
    for j in range(SEL):
        bias = jnp.where(code[:, j : j + 1] == lane, 0.0, bias)
    bias = bias.astype(BF)
    i, j = iota((256, 256), 0), iota((256, 256), 1)
    swap = one_if((j % 16) * 16 + j // 16 == i)
    for h in range(KVH):
        for c in range(OWN // 16):
            part = q_ref[c * 16 : (c + 1) * 16, h * 16 : (h + 1) * 16, :]
            turned = dot(swap, part.reshape(256, HD)).astype(BF)
            for g in range(GROUP):
                head = h * GROUP + g
                at = jnp.where(odd == 1, head, (head % LINE) * LINE + head // LINE)
                row = pl.multiple_of(at * OWN + c * 16, 16)
                qa[pl.ds(row, 16), 0:HD] = turned[g * 16 : (g + 1) * 16, :]
                qa[pl.ds(row, 16), HD : 2 * HD] = bias[h * OWN + c * 16 : h * OWN + (c + 1) * 16, :]

    point[...] = jnp.full(point.shape, FLOOR, F32)
    acc[...] = jnp.zeros(acc.shape, F32)
    first_lane = one_if(iota((TOKENS, HD), 1) == 0)
    token_page, page_lane = iota((TOKENS, HD), 0) // PAGE, iota((TOKENS, HD), 1)

    def score(block, n):
        if n == 0:
            copies[block].wait()
        keys = jnp.concatenate(
            [kv_refs[block, 0], one_if(page_lane == token_page + block * POOL)], axis=1
        )
        return dot_nt(qa[n * CHUNK : (n + 1) * CHUNK, :], keys)

    def finish(block, n, s_ref):
        here = slice(n * CHUNK, (n + 1) * CHUNK)
        s = s_ref[...]
        top = jnp.max(s, axis=1, keepdims=True) * SCALE
        old = point[here, :]
        new = jnp.maximum(jnp.broadcast_to(top.astype(BF).astype(F32), old.shape), old)
        point[here, :] = new
        p = jnp.exp2(s * (SCALE * LOG2E) - new[:, 0:1] * LOG2E).astype(BF)
        o = dot(p, jnp.concatenate([kv_refs[block, 1], first_lane], axis=1))
        fade = jnp.exp2((old - new) * LOG2E)
        acc[here, :] = acc[here, :] * jnp.concatenate([fade, fade], axis=1) + o

    chunks = HEADS * OWN // CHUNK
    steps = [(block, n) for block in range(SHARE) for n in range(chunks)]
    slots = (s_even, s_odd)
    slots[0][...] = score(*steps[0])
    for k, step in enumerate(steps):
        if k + 1 < len(steps):
            slots[(k + 1) % 2][...] = score(*steps[k + 1])
        finish(*step, slots[k % 2])

    lane = iota((OWN, HD), 1)
    for j in range(LINE):
        stats = jnp.zeros((OWN, HD), F32)
        for i in range(LINE):
            here = slice((j * LINE + i) * OWN, (j * LINE + i + 1) * OWN)
            total = acc[here, HD : HD + 1]
            total_hi = total.astype(BF).astype(F32)
            stats = jnp.where(lane == i * 8, point[here, :], stats)
            stats = jnp.where(lane == i * 8 + 1, total_hi, stats)
            stats = jnp.where(lane == i * 8 + 2, total - total_hi, stats)
            out_ref[j, i * OWN : (i + 1) * OWN, :] = acc[here, 0:HD].astype(BF)
        out_ref[j, LINE * OWN : (LINE + 1) * OWN, :] = stats.astype(BF)


def merge_kernel(r_ref, out_ref):
    kind = iota((OWN, HD), 1) % 8
    stats_of_all = []
    for rows in range(PAIR):
        sources = range(rows, LINE, PAIR)
        stats = [r_ref[src, LINE * OWN : (LINE + 1) * OWN, :].astype(F32) for src in sources]
        top = functools.reduce(jnp.maximum, stats)
        factors = [jnp.exp2((s - top) * LOG2E) for s in stats]
        total = sum(
            f * (pltpu.roll(s, HD - 1, 1) + pltpu.roll(s, HD - 2, 1))
            for f, s in zip(factors, stats)
        )
        total_hi = total.astype(BF).astype(F32)
        total_lo = pltpu.roll(total - total_hi, 2, 1)
        joint = jnp.where(kind == 1, pltpu.roll(total_hi, 1, 1), jnp.where(kind == 2, total_lo, 0.0))
        stats_of_all.append(jnp.where(kind == 0, top, joint))
        for head in range(LINE):
            acc = sum(
                f[:, head * 8 : head * 8 + 1] * r_ref[src, head * OWN : (head + 1) * OWN, :].astype(F32)
                for f, src in zip(factors, sources)
            ).astype(BF)
            out_ref[head, 0, rows * OWN : (rows + 1) * OWN, :] = acc
            out_ref[head ^ 1, 1, rows * OWN : (rows + 1) * OWN, :] = acc
    tall = jnp.concatenate(stats_of_all + [jnp.zeros((HD - HALF, HD), F32)], axis=0).T
    for head in range(LINE):
        stats = tall[head * 8 : (head + 1) * 8, :].astype(BF)
        out_ref[head, 0, HALF:SMALL, :] = stats
        out_ref[head ^ 1, 1, HALF:SMALL, :] = stats


def project_kernel(r_ref, mine_ref, theirs_hbm, out_ref, att, theirs_ref, sem):
    copy = pltpu.make_async_copy(theirs_hbm, theirs_ref, sem)
    copy.start()
    heads = []
    for head in range(PAIR):
        halves = []
        for rows in range(PAIR):
            sources = range(rows, LINE, PAIR)
            stats = [r_ref[src, head, HALF:SMALL, :].astype(F32).T[0:HALF, :] for src in sources]
            top = functools.reduce(jnp.maximum, [s[:, 0:1] for s in stats])
            factors = [jnp.exp2((s[:, 0:1] - top) * LOG2E) for s in stats]
            total = sum(f * (s[:, 1:2] + s[:, 2:3]) for f, s in zip(factors, stats))
            acc = sum(
                f * r_ref[src, head, 0:HALF, :].astype(F32) for src, f in zip(sources, factors)
            )
            halves.append((acc / total).astype(BF))
        heads.append(jnp.concatenate(halves, axis=0))
    both = jnp.concatenate(heads, axis=1)
    i, j = iota((ROWS, ROWS), 0), iota((ROWS, ROWS), 1)
    b, u = i // LINE, i % LINE
    came_from = (b % PAIR) * HALF + (u % PAIR) * OWN + (b // PAIR) * SPAN + u // PAIR
    att[...] = dot(one_if(j == came_from), both).astype(BF)

    copy.wait()
    for n in range(out_ref.shape[1] // BLOCK):
        lanes = slice(n * BLOCK, (n + 1) * BLOCK)
        weight = jnp.concatenate([mine_ref[:, lanes], theirs_ref[:, lanes]], axis=0)
        out_ref[:, lanes] = dot(att[...], weight).astype(BF)


def add_kernel(x_ref, out_ref, tmp):
    tiles = tmp.shape[0] // LINE
    half = tiles // PAIR
    for tile in range(tiles):
        lanes = slice(tile % half * 128, (tile % half + 1) * 128)
        total = sum(x_ref[src, :, lanes].astype(F32) for src in range(tile // half, LINE, PAIR))
        tmp[pl.ds(tile, LINE, stride=tiles), :] = total
    out_ref[...] = tmp[...].reshape(LINE, tiles, 128).astype(BF)


VMEM = pl.BlockSpec(memory_space=pltpu.VMEM)
ANYWHERE = pl.BlockSpec(memory_space=pl.ANY)
SMEM = pl.BlockSpec(memory_space=pltpu.SMEM)
PARAMS = pltpu.CompilerParams(vmem_limit_bytes=24 * 2**20)


def in_hbm(value):
    return pltpu.with_memory_space_constraint(value, pltpu.HBM)


def prepare(queries, ids, keys, values):
    return pl.pallas_call(
        prepare_kernel,
        out_shape=(
            jax.ShapeDtypeStruct((SPAN, SLAB, HD), BF),
            jax.ShapeDtypeStruct((2, TOKENS, HD), BF),
        ),
        in_specs=[ANYWHERE] * 4,
        out_specs=(VMEM, VMEM),
        scratch_shapes=[
            pltpu.VMEM(queries.shape, BF),
            pltpu.VMEM(ids.shape, jnp.int32),
            pltpu.VMEM((SLAB, HD), F32),
            pltpu.SemaphoreType.DMA((4,)),
        ],
        compiler_params=PARAMS,
        name="prepare",
    )(*[in_hbm(value) for value in (queries, ids, keys, values)])


def halves(side, weight):
    half = jax.ShapeDtypeStruct((HD, weight.shape[1] // PAIR), BF)
    return pl.pallas_call(
        halves_kernel,
        out_shape=(half, half),
        in_specs=[SMEM, ANYWHERE],
        out_specs=(VMEM, VMEM),
        scratch_shapes=[pltpu.SemaphoreType.DMA((2,))],
        compiler_params=PARAMS,
        name="halves",
    )(side, in_hbm(weight))


def spread(value):
    return pl.pallas_call(
        spread_kernel,
        out_shape=jax.ShapeDtypeStruct((SPAN,) + value.shape, BF),
        in_specs=[VMEM],
        out_specs=VMEM,
        compiler_params=PARAMS,
        name="spread",
    )(value)


def attend(place, got, pages):
    return pl.pallas_call(
        attend_kernel,
        out_shape=jax.ShapeDtypeStruct((LINE, (LINE + 1) * OWN, HD), BF),
        in_specs=[SMEM, VMEM] + [ANYWHERE] * SHARE,
        out_specs=VMEM,
        scratch_shapes=[
            pltpu.VMEM((SHARE, 2, TOKENS, HD), BF),
            pltpu.SemaphoreType.DMA((SHARE,)),
            pltpu.VMEM((HEADS * OWN, 2 * HD), BF),
            pltpu.VMEM((HEADS * OWN, HD), F32),
            pltpu.VMEM((HEADS * OWN, 2 * HD), F32),
            pltpu.VMEM((CHUNK, TOKENS), F32),
            pltpu.VMEM((CHUNK, TOKENS), F32),
        ],
        compiler_params=PARAMS,
        name="attend",
    )(place, got, pages[0], *[in_hbm(block) for block in pages[1:]])


def merge(parts):
    return pl.pallas_call(
        merge_kernel,
        out_shape=jax.ShapeDtypeStruct((LINE, PAIR, SMALL, HD), BF),
        in_specs=[VMEM],
        out_specs=VMEM,
        compiler_params=PARAMS,
        name="merge",
    )(parts)


def project(parts, mine, theirs):
    width = theirs.shape[1]
    return pl.pallas_call(
        project_kernel,
        out_shape=jax.ShapeDtypeStruct((ROWS, width), BF),
        in_specs=[VMEM, VMEM, ANYWHERE],
        out_specs=VMEM,
        scratch_shapes=[
            pltpu.VMEM((ROWS, PAIR * HD), BF),
            pltpu.VMEM(theirs.shape, BF),
            pltpu.SemaphoreType.DMA,
        ],
        compiler_params=PARAMS,
        name="project",
    )(parts, mine, theirs)


def add(parts):
    width = parts.shape[2] * PAIR
    return pl.pallas_call(
        add_kernel,
        out_shape=jax.ShapeDtypeStruct((LINE, width // 128, 128), BF),
        in_specs=[VMEM],
        out_specs=VMEM,
        scratch_shapes=[pltpu.VMEM((LINE * width // 128, 128), F32)],
        compiler_params=PARAMS,
        name="add",
    )(parts)


def lines(sections, first):
    groups = []
    for section in range(sections):
        base = section * LINE * LINE
        along_y = (section % 2 == 0) == first
        for other in range(LINE):
            step, start = (1, other * LINE) if along_y else (LINE, other)
            groups.append([base + start + step * k for k in range(LINE)])
    return groups


def exchange(value, groups):
    return lax.all_to_all(
        value, ("segment", "dev"), split_axis=0, concat_axis=0, axis_index_groups=groups, tiled=True
    )


def neighbours(groups):
    return [(line[k], line[k ^ 1]) for line in groups for k in range(LINE)]


def local(queries, page_ids, key_pages, value_pages, out_weight):
    count = lax.axis_size("segment")
    both = ("segment", "dev")
    one, other = lines(count, True), lines(count, False)
    one_rows = [line[rows::PAIR] for line in one for rows in range(PAIR)]
    other_rows = [line[rows::PAIR] for line in other for rows in range(PAIR)]
    odd = lax.axis_index("segment") % 2
    me = lax.axis_index("dev")
    u = jnp.where(odd == 1, me // LINE, me % LINE)
    b = jnp.where(odd == 1, me % LINE, me // LINE)
    place = []
    for block in range(SHARE):
        block_u, block_b = u ^ (block % 2), b ^ (block // 2)
        place.append(jnp.where(odd == 1, block_u * LINE + block_b, block_b * LINE + block_u))
    place = jnp.stack(place + [odd]).astype(jnp.int32)

    payload, pages = prepare(
        queries,
        page_ids.reshape(KVH, SEL),
        key_pages.reshape(TOKENS, HD),
        value_pages.reshape(TOKENS, HD),
    )
    mine, given = halves((b % PAIR).astype(jnp.int32).reshape(1), out_weight)
    near = exchange(payload, one_rows)
    pages_u = lax.ppermute(pages, both, neighbours(one))
    pages_b = lax.ppermute(pages, both, neighbours(other))
    near, came_u, _, given = lax.optimization_barrier((near, pages_u, pages_b, given))
    pages_ub = lax.ppermute(came_u, both, neighbours(other))
    got = exchange(spread(near), other_rows)
    given, got, _ = lax.optimization_barrier((given, got, pages_ub))
    theirs = lax.ppermute(given, both, neighbours(other))

    partial = attend(place, got.reshape(OWN, SLAB, HD), [pages, pages_u, pages_b, pages_ub])
    joined = merge(exchange(partial, one))
    gathered = exchange(joined, other)
    sums = project(gathered, mine, theirs)
    added = add(exchange(sums.reshape(LINE, LINE, -1), other))
    parts = exchange(added, one)
    projected = jnp.sum(parts.astype(F32), axis=0).astype(BF)
    handed = lax.ppermute(projected, "segment", [(s, (s + 1) % count) for s in range(count)])
    return handed.reshape(1, -1)


def solution(mesh):
    placed = (
        P(("segment", "dev"), None),
        P(("segment", "dev"), None, None),
        P(("segment", "dev"), None, None),
        P(("segment", "dev"), None, None),
        P(("segment", "dev"), None),
    )
    return jax.shard_map(
        local, mesh=mesh, in_specs=placed, out_specs=P(("segment", "dev"), None), check_vma=False
    )
```

```python
import functools
import math

import jax
import jax.numpy as jnp
from jax import lax
from jax.experimental import pallas as pl
from jax.experimental.pallas import tpu as pltpu
from jax.sharding import PartitionSpec as P

BF = jnp.bfloat16
F32 = jnp.float32
HEADS = 64
GROUP = 16
KVH = 4
HD = 128
ROWS = 64
POOL = 16
TOKENS = 1024
SLAB = 72
PAGE = 64
SEL = 32
LINE = 8
SHARE = 4
SPAN = 4
PAIR = 2
OWN = ROWS // SHARE
HALF = PAIR * OWN
SMALL = HALF + 8
BLOCK = 2048
CHUNK = 512
LOG2E = math.log2(math.e)
SCALE = 1.0 / math.sqrt(HD)
FAR = float(2**20)
FLOOR = -8192.0


def iota(shape, dim):
    return lax.broadcasted_iota(jnp.int32, shape, dim)


def dot(a, b):
    return lax.dot_general(a, b, (((1,), (0,)), ((), ())), preferred_element_type=F32)


def dot_nt(a, b):
    return lax.dot_general(a, b, (((1,), (1,)), ((), ())), preferred_element_type=F32)


def one_if(condition):
    return jnp.where(condition, 1.0, 0.0).astype(BF)


def prepare_kernel(q_hbm, id_hbm, out_ref, q_ref, id_ref, tmp, sems):
    copies = [
        pltpu.make_async_copy(q_hbm, q_ref, sems.at[0]),
        pltpu.make_async_copy(id_hbm, id_ref, sems.at[1]),
    ]
    for copy in copies:
        copy.start()
    for copy in copies:
        copy.wait()
    for head in range(HEADS):
        tmp[head : head + 1, :] = q_ref[:, head * HD : (head + 1) * HD].astype(F32)
    ids = id_ref[...]
    tmp[HEADS:SLAB, :] = jnp.full((SLAB - HEADS, HD), -1.0, F32)
    tmp[HEADS : HEADS + KVH, 0:SEL] = (ids // POOL).astype(F32)
    tmp[HEADS + KVH : SLAB, 0:SEL] = (ids % POOL).astype(F32)
    slab = tmp[...].astype(BF)
    for copy in range(SPAN):
        out_ref[copy, :, :] = slab


def halves_kernel(side_ref, w_hbm, mine_ref, given_ref, sems):
    width = mine_ref.shape[1]
    side = side_ref[0]
    mine = pl.ds(pl.multiple_of(side * width, width), width)
    given = pl.ds(pl.multiple_of((1 - side) * width, width), width)
    copies = [
        pltpu.make_async_copy(w_hbm.at[:, given], given_ref, sems.at[0]),
        pltpu.make_async_copy(w_hbm.at[:, mine], mine_ref, sems.at[1]),
    ]
    for copy in copies:
        copy.start()
    for copy in copies:
        copy.wait()


def pack_kernel(k_hbm, v_hbm, pages_ref, sems):
    copies = [
        pltpu.make_async_copy(k_hbm, pages_ref.at[0], sems.at[0]),
        pltpu.make_async_copy(v_hbm, pages_ref.at[1], sems.at[1]),
    ]
    for copy in copies:
        copy.start()
    for copy in copies:
        copy.wait()


def spread_kernel(x_ref, out_ref):
    for copy in range(SPAN):
        out_ref[copy, :, :, :] = x_ref[...]


def attend_kernel(place_ref, q_ref, *refs):
    kv_hbms = refs[:SHARE]
    out_ref, kv_refs, sems, qa, point, acc, s_even, s_odd = refs[SHARE:]
    copies = [
        pltpu.make_async_copy(kv_hbms[block], kv_refs.at[block], sems.at[block])
        for block in range(SHARE)
    ]
    for copy in copies:
        copy.start()
    odd = place_ref[SHARE]
    ids = q_ref[:, HEADS:SLAB, :].astype(F32).reshape(OWN * 8, HD).astype(BF)
    i, j = iota((KVH * OWN, OWN * 8), 0), iota((KVH * OWN, OWN * 8), 1)
    first = (i % OWN) * 8 + i // OWN
    owner = dot(one_if(j == first), ids)
    slot = dot(one_if(j == first + KVH), ids)
    code = jnp.full((KVH * OWN, HD), -1.0, F32)
    for block in range(SHARE):
        code = jnp.where(owner == place_ref[block].astype(F32), slot + float(block * POOL), code)
    lane = iota((KVH * OWN, HD), 1).astype(F32)
    bias = jnp.full((KVH * OWN, HD), -FAR, F32)
    for j in range(SEL):
        bias = jnp.where(code[:, j : j + 1] == lane, 0.0, bias)
    bias = bias.astype(BF)
    i, j = iota((256, 256), 0), iota((256, 256), 1)
    swap = one_if((j % 16) * 16 + j // 16 == i)
    for h in range(KVH):
        for c in range(OWN // 16):
            part = q_ref[c * 16 : (c + 1) * 16, h * 16 : (h + 1) * 16, :]
            turned = dot(swap, part.reshape(256, HD)).astype(BF)
            for g in range(GROUP):
                head = h * GROUP + g
                at = jnp.where(odd == 1, head, (head % LINE) * LINE + head // LINE)
                row = pl.multiple_of(at * OWN + c * 16, 16)
                qa[pl.ds(row, 16), 0:HD] = turned[g * 16 : (g + 1) * 16, :]
                qa[pl.ds(row, 16), HD : 2 * HD] = bias[h * OWN + c * 16 : h * OWN + (c + 1) * 16, :]

    point[...] = jnp.full(point.shape, FLOOR, F32)
    acc[...] = jnp.zeros(acc.shape, F32)
    first_lane = one_if(iota((TOKENS, HD), 1) == 0)
    token_page, page_lane = iota((TOKENS, HD), 0) // PAGE, iota((TOKENS, HD), 1)

    def score(block, n):
        if n == 0:
            copies[block].wait()
        keys = jnp.concatenate(
            [kv_refs[block, 0], one_if(page_lane == token_page + block * POOL)], axis=1
        )
        return dot_nt(qa[n * CHUNK : (n + 1) * CHUNK, :], keys)

    def finish(block, n, s_ref):
        here = slice(n * CHUNK, (n + 1) * CHUNK)
        s = s_ref[...]
        top = jnp.max(s, axis=1, keepdims=True) * SCALE
        old = point[here, :]
        new = jnp.maximum(jnp.broadcast_to(top.astype(BF).astype(F32), old.shape), old)
        point[here, :] = new
        p = jnp.exp2(s * (SCALE * LOG2E) - new[:, 0:1] * LOG2E).astype(BF)
        o = dot(p, jnp.concatenate([kv_refs[block, 1], first_lane], axis=1))
        fade = jnp.exp2((old - new) * LOG2E)
        acc[here, :] = acc[here, :] * jnp.concatenate([fade, fade], axis=1) + o

    chunks = HEADS * OWN // CHUNK
    steps = [(block, n) for block in range(SHARE) for n in range(chunks)]
    slots = (s_even, s_odd)
    slots[0][...] = score(*steps[0])
    for k, step in enumerate(steps):
        if k + 1 < len(steps):
            slots[(k + 1) % 2][...] = score(*steps[k + 1])
        finish(*step, slots[k % 2])

    lane = iota((OWN, HD), 1)
    for j in range(LINE):
        stats = jnp.zeros((OWN, HD), F32)
        for i in range(LINE):
            here = slice((j * LINE + i) * OWN, (j * LINE + i + 1) * OWN)
            total = acc[here, HD : HD + 1]
            total_hi = total.astype(BF).astype(F32)
            stats = jnp.where(lane == i * 8, point[here, :], stats)
            stats = jnp.where(lane == i * 8 + 1, total_hi, stats)
            stats = jnp.where(lane == i * 8 + 2, total - total_hi, stats)
            out_ref[j, i * OWN : (i + 1) * OWN, :] = acc[here, 0:HD].astype(BF)
        out_ref[j, LINE * OWN : (LINE + 1) * OWN, :] = stats.astype(BF)


def merge_kernel(r_ref, out_ref):
    kind = iota((OWN, HD), 1) % 8
    stats_of_all = []
    for rows in range(PAIR):
        sources = range(rows, LINE, PAIR)
        stats = [r_ref[src, LINE * OWN : (LINE + 1) * OWN, :].astype(F32) for src in sources]
        top = functools.reduce(jnp.maximum, stats)
        factors = [jnp.exp2((s - top) * LOG2E) for s in stats]
        total = sum(
            f * (pltpu.roll(s, HD - 1, 1) + pltpu.roll(s, HD - 2, 1))
            for f, s in zip(factors, stats)
        )
        total_hi = total.astype(BF).astype(F32)
        total_lo = pltpu.roll(total - total_hi, 2, 1)
        joint = jnp.where(kind == 1, pltpu.roll(total_hi, 1, 1), jnp.where(kind == 2, total_lo, 0.0))
        stats_of_all.append(jnp.where(kind == 0, top, joint))
        for head in range(LINE):
            acc = sum(
                f[:, head * 8 : head * 8 + 1] * r_ref[src, head * OWN : (head + 1) * OWN, :].astype(F32)
                for f, src in zip(factors, sources)
            ).astype(BF)
            out_ref[head, 0, rows * OWN : (rows + 1) * OWN, :] = acc
            out_ref[head ^ 1, 1, rows * OWN : (rows + 1) * OWN, :] = acc
    tall = jnp.concatenate(stats_of_all + [jnp.zeros((HD - HALF, HD), F32)], axis=0).T
    for head in range(LINE):
        stats = tall[head * 8 : (head + 1) * 8, :].astype(BF)
        out_ref[head, 0, HALF:SMALL, :] = stats
        out_ref[head ^ 1, 1, HALF:SMALL, :] = stats


def project_kernel(r_ref, mine_ref, theirs_hbm, out_ref, att, theirs_ref, sem):
    copy = pltpu.make_async_copy(theirs_hbm, theirs_ref, sem)
    copy.start()
    heads = []
    for head in range(PAIR):
        halves = []
        for rows in range(PAIR):
            sources = range(rows, LINE, PAIR)
            stats = [r_ref[src, head, HALF:SMALL, :].astype(F32).T[0:HALF, :] for src in sources]
            top = functools.reduce(jnp.maximum, [s[:, 0:1] for s in stats])
            factors = [jnp.exp2((s[:, 0:1] - top) * LOG2E) for s in stats]
            total = sum(f * (s[:, 1:2] + s[:, 2:3]) for f, s in zip(factors, stats))
            acc = sum(
                f * r_ref[src, head, 0:HALF, :].astype(F32) for src, f in zip(sources, factors)
            )
            halves.append((acc / total).astype(BF))
        heads.append(jnp.concatenate(halves, axis=0))
    both = jnp.concatenate(heads, axis=1)
    i, j = iota((ROWS, ROWS), 0), iota((ROWS, ROWS), 1)
    b, u = i // LINE, i % LINE
    came_from = (b % PAIR) * HALF + (u % PAIR) * OWN + (b // PAIR) * SPAN + u // PAIR
    att[...] = dot(one_if(j == came_from), both).astype(BF)

    copy.wait()
    for n in range(out_ref.shape[1] // BLOCK):
        lanes = slice(n * BLOCK, (n + 1) * BLOCK)
        weight = jnp.concatenate([mine_ref[:, lanes], theirs_ref[:, lanes]], axis=0)
        out_ref[:, lanes] = dot(att[...], weight).astype(BF)


def add_kernel(x_ref, out_ref, tmp):
    tiles = tmp.shape[0] // LINE
    half = tiles // PAIR
    for tile in range(tiles):
        lanes = slice(tile % half * 128, (tile % half + 1) * 128)
        total = sum(x_ref[src, :, lanes].astype(F32) for src in range(tile // half, LINE, PAIR))
        tmp[pl.ds(tile, LINE, stride=tiles), :] = total
    out_ref[...] = tmp[...].reshape(LINE, tiles, 128).astype(BF)


VMEM = pl.BlockSpec(memory_space=pltpu.VMEM)
ANYWHERE = pl.BlockSpec(memory_space=pl.ANY)
SMEM = pl.BlockSpec(memory_space=pltpu.SMEM)
PARAMS = pltpu.CompilerParams(vmem_limit_bytes=24 * 2**20)


def in_hbm(value):
    return pltpu.with_memory_space_constraint(value, pltpu.HBM)


def prepare(queries, ids):
    return pl.pallas_call(
        prepare_kernel,
        out_shape=jax.ShapeDtypeStruct((SPAN, SLAB, HD), BF),
        in_specs=[ANYWHERE] * 2,
        out_specs=VMEM,
        scratch_shapes=[
            pltpu.VMEM(queries.shape, BF),
            pltpu.VMEM(ids.shape, jnp.int32),
            pltpu.VMEM((SLAB, HD), F32),
            pltpu.SemaphoreType.DMA((2,)),
        ],
        compiler_params=PARAMS,
        name="prepare",
    )(in_hbm(queries), in_hbm(ids))


def pack(keys, values):
    return pl.pallas_call(
        pack_kernel,
        out_shape=jax.ShapeDtypeStruct((2,) + keys.shape, BF),
        in_specs=[ANYWHERE] * 2,
        out_specs=VMEM,
        scratch_shapes=[pltpu.SemaphoreType.DMA((2,))],
        compiler_params=PARAMS,
        name="pack",
    )(in_hbm(keys), in_hbm(values))


def halves(side, weight):
    half = jax.ShapeDtypeStruct((HD, weight.shape[1] // PAIR), BF)
    return pl.pallas_call(
        halves_kernel,
        out_shape=(half, half),
        in_specs=[SMEM, ANYWHERE],
        out_specs=(VMEM, VMEM),
        scratch_shapes=[pltpu.SemaphoreType.DMA((2,))],
        compiler_params=PARAMS,
        name="halves",
    )(side, in_hbm(weight))


def spread(value):
    return pl.pallas_call(
        spread_kernel,
        out_shape=jax.ShapeDtypeStruct((SPAN,) + value.shape, BF),
        in_specs=[VMEM],
        out_specs=VMEM,
        compiler_params=PARAMS,
        name="spread",
    )(value)


def attend(place, got, pages):
    return pl.pallas_call(
        attend_kernel,
        out_shape=jax.ShapeDtypeStruct((LINE, (LINE + 1) * OWN, HD), BF),
        in_specs=[SMEM, VMEM] + [ANYWHERE] * SHARE,
        out_specs=VMEM,
        scratch_shapes=[
            pltpu.VMEM((SHARE, 2, TOKENS, HD), BF),
            pltpu.SemaphoreType.DMA((SHARE,)),
            pltpu.VMEM((HEADS * OWN, 2 * HD), BF),
            pltpu.VMEM((HEADS * OWN, HD), F32),
            pltpu.VMEM((HEADS * OWN, 2 * HD), F32),
            pltpu.VMEM((CHUNK, TOKENS), F32),
            pltpu.VMEM((CHUNK, TOKENS), F32),
        ],
        compiler_params=PARAMS,
        name="attend",
    )(place, got, pages[0], *[in_hbm(block) for block in pages[1:]])


def merge(parts):
    return pl.pallas_call(
        merge_kernel,
        out_shape=jax.ShapeDtypeStruct((LINE, PAIR, SMALL, HD), BF),
        in_specs=[VMEM],
        out_specs=VMEM,
        compiler_params=PARAMS,
        name="merge",
    )(parts)


def project(parts, mine, theirs):
    width = theirs.shape[1]
    return pl.pallas_call(
        project_kernel,
        out_shape=jax.ShapeDtypeStruct((ROWS, width), BF),
        in_specs=[VMEM, VMEM, ANYWHERE],
        out_specs=VMEM,
        scratch_shapes=[
            pltpu.VMEM((ROWS, PAIR * HD), BF),
            pltpu.VMEM(theirs.shape, BF),
            pltpu.SemaphoreType.DMA,
        ],
        compiler_params=PARAMS,
        name="project",
    )(parts, mine, theirs)


def add(parts):
    width = parts.shape[2] * PAIR
    return pl.pallas_call(
        add_kernel,
        out_shape=jax.ShapeDtypeStruct((LINE, width // 128, 128), BF),
        in_specs=[VMEM],
        out_specs=VMEM,
        scratch_shapes=[pltpu.VMEM((LINE * width // 128, 128), F32)],
        compiler_params=PARAMS,
        name="add",
    )(parts)


def lines(sections, first):
    groups = []
    for section in range(sections):
        base = section * LINE * LINE
        along_y = (section % 2 == 0) == first
        for other in range(LINE):
            step, start = (1, other * LINE) if along_y else (LINE, other)
            groups.append([base + start + step * k for k in range(LINE)])
    return groups


def exchange(value, groups):
    return lax.all_to_all(
        value, ("segment", "dev"), split_axis=0, concat_axis=0, axis_index_groups=groups, tiled=True
    )


def neighbours(groups):
    return [(line[k], line[k ^ 1]) for line in groups for k in range(LINE)]


def diagonal(groups):
    pairs = []
    for number, line in enumerate(groups):
        pairs += [(line[k], groups[number ^ 1][k ^ 1]) for k in range(LINE)]
    return pairs


def local(queries, page_ids, key_pages, value_pages, out_weight):
    count = lax.axis_size("segment")
    both = ("segment", "dev")
    one, other = lines(count, True), lines(count, False)
    one_rows = [line[rows::PAIR] for line in one for rows in range(PAIR)]
    other_rows = [line[rows::PAIR] for line in other for rows in range(PAIR)]
    odd = lax.axis_index("segment") % 2
    me = lax.axis_index("dev")
    u = jnp.where(odd == 1, me // LINE, me % LINE)
    b = jnp.where(odd == 1, me % LINE, me // LINE)
    place = []
    for block in range(SHARE):
        block_u, block_b = u ^ (block % 2), b ^ (block // 2)
        place.append(jnp.where(odd == 1, block_u * LINE + block_b, block_b * LINE + block_u))
    place = jnp.stack(place + [odd]).astype(jnp.int32)

    payload = prepare(queries, page_ids.reshape(KVH, SEL))
    near = exchange(payload, one_rows)
    keys, values = key_pages.reshape(TOKENS, HD), value_pages.reshape(TOKENS, HD)
    pages = pack(keys, values)
    mine, given = halves((b % PAIR).astype(jnp.int32).reshape(1), out_weight)
    pages_u = lax.ppermute(pages, both, neighbours(one))
    pages_b = lax.ppermute(pages, both, neighbours(other))
    pages_ub = lax.ppermute(pages, both, diagonal(one))
    near, given = lax.optimization_barrier((near, given))
    got = exchange(spread(near), other_rows)
    given, got, *_ = lax.optimization_barrier((given, got, pages_u, pages_b, pages_ub))
    theirs = lax.ppermute(given, both, neighbours(other))

    partial = attend(place, got.reshape(OWN, SLAB, HD), [pages, pages_u, pages_b, pages_ub])
    joined = merge(exchange(partial, one))
    gathered = exchange(joined, other)
    sums = project(gathered, mine, theirs)
    added = add(exchange(sums.reshape(LINE, LINE, -1), other))
    parts = exchange(added, one)
    projected = jnp.sum(parts.astype(F32), axis=0).astype(BF)
    handed = lax.ppermute(projected, "segment", [(s, (s + 1) % count) for s in range(count)])
    return handed.reshape(1, -1)


def solution(mesh):
    placed = (
        P(("segment", "dev"), None),
        P(("segment", "dev"), None, None),
        P(("segment", "dev"), None, None),
        P(("segment", "dev"), None, None),
        P(("segment", "dev"), None),
    )
    return jax.shard_map(
        local, mesh=mesh, in_specs=placed, out_specs=P(("segment", "dev"), None), check_vma=False
    )
```

```python
import functools
import math

import jax
import jax.numpy as jnp
from jax import lax
from jax.experimental import pallas as pl
from jax.experimental.pallas import tpu as pltpu
from jax.sharding import PartitionSpec as P

BF = jnp.bfloat16
F32 = jnp.float32
HEADS = 64
GROUP = 16
KVH = 4
HD = 128
ROWS = 64
POOL = 16
TOKENS = 1024
SLAB = 72
PAGE = 64
SEL = 32
LINE = 8
SHARE = 4
SPAN = 4
PAIR = 2
OWN = ROWS // SHARE
HALF = PAIR * OWN
SMALL = HALF + 8
BLOCK = 2048
CHUNK = 512
LOG2E = math.log2(math.e)
SCALE = 1.0 / math.sqrt(HD)
FAR = float(2**20)
FLOOR = -8192.0


def iota(shape, dim):
    return lax.broadcasted_iota(jnp.int32, shape, dim)


def dot(a, b):
    return lax.dot_general(a, b, (((1,), (0,)), ((), ())), preferred_element_type=F32)


def dot_nt(a, b):
    return lax.dot_general(a, b, (((1,), (1,)), ((), ())), preferred_element_type=F32)


def one_if(condition):
    return jnp.where(condition, 1.0, 0.0).astype(BF)


def prepare_kernel(q_hbm, id_hbm, k_hbm, v_hbm, out_ref, pages_ref, q_ref, id_ref, tmp, sems):
    copies = [
        pltpu.make_async_copy(q_hbm, q_ref, sems.at[0]),
        pltpu.make_async_copy(id_hbm, id_ref, sems.at[1]),
        pltpu.make_async_copy(k_hbm, pages_ref.at[0], sems.at[2]),
        pltpu.make_async_copy(v_hbm, pages_ref.at[1], sems.at[3]),
    ]
    for copy in copies:
        copy.start()
    copies[0].wait()
    copies[1].wait()
    for head in range(HEADS):
        tmp[head : head + 1, :] = q_ref[:, head * HD : (head + 1) * HD].astype(F32)
    ids = id_ref[...]
    tmp[HEADS:SLAB, :] = jnp.full((SLAB - HEADS, HD), -1.0, F32)
    tmp[HEADS : HEADS + KVH, 0:SEL] = (ids // POOL).astype(F32)
    tmp[HEADS + KVH : SLAB, 0:SEL] = (ids % POOL).astype(F32)
    slab = tmp[...].astype(BF)
    for copy in range(SPAN):
        out_ref[copy, :, :] = slab
    copies[2].wait()
    copies[3].wait()


def halves_kernel(side_ref, w_hbm, mine_ref, given_ref, sems):
    width = mine_ref.shape[1]
    side = side_ref[0]
    mine = pl.ds(pl.multiple_of(side * width, width), width)
    given = pl.ds(pl.multiple_of((1 - side) * width, width), width)
    copies = [
        pltpu.make_async_copy(w_hbm.at[:, given], given_ref, sems.at[0]),
        pltpu.make_async_copy(w_hbm.at[:, mine], mine_ref, sems.at[1]),
    ]
    for copy in copies:
        copy.start()
    for copy in copies:
        copy.wait()


def spread_kernel(x_ref, out_ref):
    for copy in range(SPAN):
        out_ref[copy, :, :, :] = x_ref[...]


def attend_kernel(place_ref, q_ref, *refs):
    own_ref, kv_hbms = refs[0], refs[1:SHARE]
    out_ref, others, sems, qa, point, acc, s_even, s_odd = refs[SHARE:]
    copies = [
        pltpu.make_async_copy(kv_hbms[block], others.at[block], sems.at[block])
        for block in range(SHARE - 1)
    ]
    for copy in copies:
        copy.start()
    kv_refs = [own_ref] + [others.at[block] for block in range(SHARE - 1)]
    odd = place_ref[SHARE]
    ids = q_ref[:, HEADS:SLAB, :].astype(F32).reshape(OWN * 8, HD).astype(BF)
    i, j = iota((KVH * OWN, OWN * 8), 0), iota((KVH * OWN, OWN * 8), 1)
    first = (i % OWN) * 8 + i // OWN
    owner = dot(one_if(j == first), ids)
    slot = dot(one_if(j == first + KVH), ids)
    code = jnp.full((KVH * OWN, HD), -1.0, F32)
    for block in range(SHARE):
        code = jnp.where(owner == place_ref[block].astype(F32), slot + float(block * POOL), code)
    lane = iota((KVH * OWN, HD), 1).astype(F32)
    bias = jnp.full((KVH * OWN, HD), -FAR, F32)
    for j in range(SEL):
        bias = jnp.where(code[:, j : j + 1] == lane, 0.0, bias)
    bias = bias.astype(BF)
    i, j = iota((256, 256), 0), iota((256, 256), 1)
    swap = one_if((j % 16) * 16 + j // 16 == i)
    for h in range(KVH):
        for c in range(OWN // 16):
            part = q_ref[c * 16 : (c + 1) * 16, h * 16 : (h + 1) * 16, :]
            turned = dot(swap, part.reshape(256, HD)).astype(BF)
            for g in range(GROUP):
                head = h * GROUP + g
                at = jnp.where(odd == 1, head, (head % LINE) * LINE + head // LINE)
                row = pl.multiple_of(at * OWN + c * 16, 16)
                qa[pl.ds(row, 16), 0:HD] = turned[g * 16 : (g + 1) * 16, :]
                qa[pl.ds(row, 16), HD : 2 * HD] = bias[h * OWN + c * 16 : h * OWN + (c + 1) * 16, :]

    point[...] = jnp.full(point.shape, FLOOR, F32)
    acc[...] = jnp.zeros(acc.shape, F32)
    first_lane = one_if(iota((TOKENS, HD), 1) == 0)
    token_page, page_lane = iota((TOKENS, HD), 0) // PAGE, iota((TOKENS, HD), 1)

    def score(block, n):
        if (block, n) == (1, 0):
            for copy in copies:
                copy.wait()
        keys = jnp.concatenate(
            [kv_refs[block][0], one_if(page_lane == token_page + block * POOL)], axis=1
        )
        return dot_nt(qa[n * CHUNK : (n + 1) * CHUNK, :], keys)

    def finish(block, n, s_ref):
        here = slice(n * CHUNK, (n + 1) * CHUNK)
        s = s_ref[...]
        top = jnp.max(s, axis=1, keepdims=True) * SCALE
        old = point[here, :]
        new = jnp.maximum(jnp.broadcast_to(top.astype(BF).astype(F32), old.shape), old)
        point[here, :] = new
        p = jnp.exp2(s * (SCALE * LOG2E) - new[:, 0:1] * LOG2E).astype(BF)
        o = dot(p, jnp.concatenate([kv_refs[block][1], first_lane], axis=1))
        fade = jnp.exp2((old - new) * LOG2E)
        acc[here, :] = acc[here, :] * jnp.concatenate([fade, fade], axis=1) + o

    chunks = HEADS * OWN // CHUNK
    steps = [(block, n) for block in range(SHARE) for n in range(chunks)]
    slots = (s_even, s_odd)
    slots[0][...] = score(*steps[0])
    for k, step in enumerate(steps):
        if k + 1 < len(steps):
            slots[(k + 1) % 2][...] = score(*steps[k + 1])
        finish(*step, slots[k % 2])

    lane = iota((OWN, HD), 1)
    for j in range(LINE):
        stats = jnp.zeros((OWN, HD), F32)
        for i in range(LINE):
            here = slice((j * LINE + i) * OWN, (j * LINE + i + 1) * OWN)
            total = acc[here, HD : HD + 1]
            total_hi = total.astype(BF).astype(F32)
            stats = jnp.where(lane == i * 8, point[here, :], stats)
            stats = jnp.where(lane == i * 8 + 1, total_hi, stats)
            stats = jnp.where(lane == i * 8 + 2, total - total_hi, stats)
            out_ref[j, i * OWN : (i + 1) * OWN, :] = acc[here, 0:HD].astype(BF)
        out_ref[j, LINE * OWN : (LINE + 1) * OWN, :] = stats.astype(BF)


def merge_kernel(r_ref, out_ref):
    kind = iota((OWN, HD), 1) % 8
    stats_of_all = []
    for rows in range(PAIR):
        sources = range(rows, LINE, PAIR)
        stats = [r_ref[src, LINE * OWN : (LINE + 1) * OWN, :].astype(F32) for src in sources]
        top = functools.reduce(jnp.maximum, stats)
        factors = [jnp.exp2((s - top) * LOG2E) for s in stats]
        total = sum(
            f * (pltpu.roll(s, HD - 1, 1) + pltpu.roll(s, HD - 2, 1))
            for f, s in zip(factors, stats)
        )
        total_hi = total.astype(BF).astype(F32)
        total_lo = pltpu.roll(total - total_hi, 2, 1)
        joint = jnp.where(kind == 1, pltpu.roll(total_hi, 1, 1), jnp.where(kind == 2, total_lo, 0.0))
        stats_of_all.append(jnp.where(kind == 0, top, joint))
        for head in range(LINE):
            acc = sum(
                f[:, head * 8 : head * 8 + 1] * r_ref[src, head * OWN : (head + 1) * OWN, :].astype(F32)
                for f, src in zip(factors, sources)
            ).astype(BF)
            out_ref[head, 0, rows * OWN : (rows + 1) * OWN, :] = acc
            out_ref[head ^ 1, 1, rows * OWN : (rows + 1) * OWN, :] = acc
    tall = jnp.concatenate(stats_of_all + [jnp.zeros((HD - HALF, HD), F32)], axis=0).T
    for head in range(LINE):
        stats = tall[head * 8 : (head + 1) * 8, :].astype(BF)
        out_ref[head, 0, HALF:SMALL, :] = stats
        out_ref[head ^ 1, 1, HALF:SMALL, :] = stats


def project_kernel(r_ref, mine_ref, theirs_hbm, out_ref, att, theirs_ref, sem):
    copy = pltpu.make_async_copy(theirs_hbm, theirs_ref, sem)
    copy.start()
    heads = []
    for head in range(PAIR):
        halves = []
        for rows in range(PAIR):
            sources = range(rows, LINE, PAIR)
            stats = [r_ref[src, head, HALF:SMALL, :].astype(F32).T[0:HALF, :] for src in sources]
            top = functools.reduce(jnp.maximum, [s[:, 0:1] for s in stats])
            factors = [jnp.exp2((s[:, 0:1] - top) * LOG2E) for s in stats]
            total = sum(f * (s[:, 1:2] + s[:, 2:3]) for f, s in zip(factors, stats))
            acc = sum(
                f * r_ref[src, head, 0:HALF, :].astype(F32) for src, f in zip(sources, factors)
            )
            halves.append((acc / total).astype(BF))
        heads.append(jnp.concatenate(halves, axis=0))
    both = jnp.concatenate(heads, axis=1)
    i, j = iota((ROWS, ROWS), 0), iota((ROWS, ROWS), 1)
    b, u = i // LINE, i % LINE
    came_from = (b % PAIR) * HALF + (u % PAIR) * OWN + (b // PAIR) * SPAN + u // PAIR
    att[...] = dot(one_if(j == came_from), both).astype(BF)

    copy.wait()
    for n in range(out_ref.shape[1] // BLOCK):
        lanes = slice(n * BLOCK, (n + 1) * BLOCK)
        weight = jnp.concatenate([mine_ref[:, lanes], theirs_ref[:, lanes]], axis=0)
        out_ref[:, lanes] = dot(att[...], weight).astype(BF)


def add_kernel(x_ref, out_ref, tmp):
    tiles = tmp.shape[0] // LINE
    half = tiles // PAIR
    for tile in range(tiles):
        lanes = slice(tile % half * 128, (tile % half + 1) * 128)
        total = sum(x_ref[src, :, lanes].astype(F32) for src in range(tile // half, LINE, PAIR))
        tmp[pl.ds(tile, LINE, stride=tiles), :] = total
    out_ref[...] = tmp[...].reshape(LINE, tiles, 128).astype(BF)


VMEM = pl.BlockSpec(memory_space=pltpu.VMEM)
ANYWHERE = pl.BlockSpec(memory_space=pl.ANY)
SMEM = pl.BlockSpec(memory_space=pltpu.SMEM)
PARAMS = pltpu.CompilerParams(vmem_limit_bytes=24 * 2**20)


def in_hbm(value):
    return pltpu.with_memory_space_constraint(value, pltpu.HBM)


def prepare(queries, ids, keys, values):
    return pl.pallas_call(
        prepare_kernel,
        out_shape=(
            jax.ShapeDtypeStruct((SPAN, SLAB, HD), BF),
            jax.ShapeDtypeStruct((2, TOKENS, HD), BF),
        ),
        in_specs=[ANYWHERE] * 4,
        out_specs=(VMEM, VMEM),
        scratch_shapes=[
            pltpu.VMEM(queries.shape, BF),
            pltpu.VMEM(ids.shape, jnp.int32),
            pltpu.VMEM((SLAB, HD), F32),
            pltpu.SemaphoreType.DMA((4,)),
        ],
        compiler_params=PARAMS,
        name="prepare",
    )(*[in_hbm(value) for value in (queries, ids, keys, values)])


def halves(side, weight):
    half = jax.ShapeDtypeStruct((HD, weight.shape[1] // PAIR), BF)
    return pl.pallas_call(
        halves_kernel,
        out_shape=(half, half),
        in_specs=[SMEM, ANYWHERE],
        out_specs=(VMEM, VMEM),
        scratch_shapes=[pltpu.SemaphoreType.DMA((2,))],
        compiler_params=PARAMS,
        name="halves",
    )(side, in_hbm(weight))


def spread(value):
    return pl.pallas_call(
        spread_kernel,
        out_shape=jax.ShapeDtypeStruct((SPAN,) + value.shape, BF),
        in_specs=[VMEM],
        out_specs=VMEM,
        compiler_params=PARAMS,
        name="spread",
    )(value)


def attend(place, got, pages):
    return pl.pallas_call(
        attend_kernel,
        out_shape=jax.ShapeDtypeStruct((LINE, (LINE + 1) * OWN, HD), BF),
        in_specs=[SMEM, VMEM, VMEM] + [ANYWHERE] * (SHARE - 1),
        out_specs=VMEM,
        scratch_shapes=[
            pltpu.VMEM((SHARE - 1, 2, TOKENS, HD), BF),
            pltpu.SemaphoreType.DMA((SHARE - 1,)),
            pltpu.VMEM((HEADS * OWN, 2 * HD), BF),
            pltpu.VMEM((HEADS * OWN, HD), F32),
            pltpu.VMEM((HEADS * OWN, 2 * HD), F32),
            pltpu.VMEM((CHUNK, TOKENS), F32),
            pltpu.VMEM((CHUNK, TOKENS), F32),
        ],
        compiler_params=PARAMS,
        name="attend",
    )(place, got, pages[0], *[in_hbm(block) for block in pages[1:]])


def merge(parts):
    return pl.pallas_call(
        merge_kernel,
        out_shape=jax.ShapeDtypeStruct((LINE, PAIR, SMALL, HD), BF),
        in_specs=[VMEM],
        out_specs=VMEM,
        compiler_params=PARAMS,
        name="merge",
    )(parts)


def project(parts, mine, theirs):
    width = theirs.shape[1]
    return pl.pallas_call(
        project_kernel,
        out_shape=jax.ShapeDtypeStruct((ROWS, width), BF),
        in_specs=[VMEM, VMEM, ANYWHERE],
        out_specs=VMEM,
        scratch_shapes=[
            pltpu.VMEM((ROWS, PAIR * HD), BF),
            pltpu.VMEM(theirs.shape, BF),
            pltpu.SemaphoreType.DMA,
        ],
        compiler_params=PARAMS,
        name="project",
    )(parts, mine, theirs)


def add(parts):
    width = parts.shape[2] * PAIR
    return pl.pallas_call(
        add_kernel,
        out_shape=jax.ShapeDtypeStruct((LINE, width // 128, 128), BF),
        in_specs=[VMEM],
        out_specs=VMEM,
        scratch_shapes=[pltpu.VMEM((LINE * width // 128, 128), F32)],
        compiler_params=PARAMS,
        name="add",
    )(parts)


def lines(sections, first):
    groups = []
    for section in range(sections):
        base = section * LINE * LINE
        along_y = (section % 2 == 0) == first
        for other in range(LINE):
            step, start = (1, other * LINE) if along_y else (LINE, other)
            groups.append([base + start + step * k for k in range(LINE)])
    return groups


def exchange(value, groups):
    return lax.all_to_all(
        value, ("segment", "dev"), split_axis=0, concat_axis=0, axis_index_groups=groups, tiled=True
    )


def neighbours(groups):
    return [(line[k], line[k ^ 1]) for line in groups for k in range(LINE)]


def local(queries, page_ids, key_pages, value_pages, out_weight):
    count = lax.axis_size("segment")
    both = ("segment", "dev")
    one, other = lines(count, True), lines(count, False)
    one_rows = [line[rows::PAIR] for line in one for rows in range(PAIR)]
    other_rows = [line[rows::PAIR] for line in other for rows in range(PAIR)]
    odd = lax.axis_index("segment") % 2
    me = lax.axis_index("dev")
    u = jnp.where(odd == 1, me // LINE, me % LINE)
    b = jnp.where(odd == 1, me % LINE, me // LINE)
    place = []
    for block in range(SHARE):
        block_u, block_b = u ^ (block % 2), b ^ (block // 2)
        place.append(jnp.where(odd == 1, block_u * LINE + block_b, block_b * LINE + block_u))
    place = jnp.stack(place + [odd]).astype(jnp.int32)

    payload, pages = prepare(
        queries,
        page_ids.reshape(KVH, SEL),
        key_pages.reshape(TOKENS, HD),
        value_pages.reshape(TOKENS, HD),
    )
    mine, given = halves((b % PAIR).astype(jnp.int32).reshape(1), out_weight)
    near = exchange(payload, one_rows)
    pages_u = lax.ppermute(pages, both, neighbours(one))
    pages_b = lax.ppermute(pages, both, neighbours(other))
    near, came_u, _, given = lax.optimization_barrier((near, pages_u, pages_b, given))
    pages_ub = lax.ppermute(came_u, both, neighbours(other))
    got = exchange(spread(near), other_rows)
    given, got, _ = lax.optimization_barrier((given, got, pages_ub))
    theirs = lax.ppermute(given, both, neighbours(other))

    partial = attend(place, got.reshape(OWN, SLAB, HD), [pages, pages_u, pages_b, pages_ub])
    joined = merge(exchange(partial, one))
    gathered = exchange(joined, other)
    sums = project(gathered, mine, theirs)
    added = add(exchange(sums.reshape(LINE, LINE, -1), other))
    parts = exchange(added, one)
    projected = jnp.sum(parts.astype(F32), axis=0).astype(BF)
    handed = lax.ppermute(projected, "segment", [(s, (s + 1) % count) for s in range(count)])
    return handed.reshape(1, -1)


def solution(mesh):
    placed = (
        P(("segment", "dev"), None),
        P(("segment", "dev"), None, None),
        P(("segment", "dev"), None, None),
        P(("segment", "dev"), None, None),
        P(("segment", "dev"), None),
    )
    return jax.shard_map(
        local, mesh=mesh, in_specs=placed, out_specs=P(("segment", "dev"), None), check_vma=False
    )
```

```python
import functools
import math

import jax
import jax.numpy as jnp
from jax import lax
from jax.experimental import pallas as pl
from jax.experimental.pallas import tpu as pltpu
from jax.sharding import PartitionSpec as P

BF = jnp.bfloat16
F32 = jnp.float32
HEADS = 64
GROUP = 16
KVH = 4
HD = 128
ROWS = 64
POOL = 16
TOKENS = 1024
SLAB = 72
PAGE = 64
SEL = 32
LINE = 8
SHARE = 4
SPAN = 4
PAIR = 2
OWN = ROWS // SHARE
HALF = PAIR * OWN
SMALL = HALF + 8
BLOCK = 2048
CHUNK = 512
LOG2E = math.log2(math.e)
SCALE = 1.0 / math.sqrt(HD)
FAR = float(2**20)
FLOOR = -8192.0


def iota(shape, dim):
    return lax.broadcasted_iota(jnp.int32, shape, dim)


def dot(a, b):
    return lax.dot_general(a, b, (((1,), (0,)), ((), ())), preferred_element_type=F32)


def dot_nt(a, b):
    return lax.dot_general(a, b, (((1,), (1,)), ((), ())), preferred_element_type=F32)


def one_if(condition):
    return jnp.where(condition, 1.0, 0.0).astype(BF)


def prepare_kernel(q_hbm, id_hbm, k_hbm, v_hbm, out_ref, pages_ref, q_ref, id_ref, tmp, sems):
    copies = [
        pltpu.make_async_copy(q_hbm, q_ref, sems.at[0]),
        pltpu.make_async_copy(id_hbm, id_ref, sems.at[1]),
        pltpu.make_async_copy(k_hbm, pages_ref.at[0], sems.at[2]),
        pltpu.make_async_copy(v_hbm, pages_ref.at[1], sems.at[3]),
    ]
    for copy in copies:
        copy.start()
    copies[0].wait()
    copies[1].wait()
    for head in range(HEADS):
        tmp[head : head + 1, :] = q_ref[:, head * HD : (head + 1) * HD].astype(F32)
    ids = id_ref[...]
    tmp[HEADS:SLAB, :] = jnp.full((SLAB - HEADS, HD), -1.0, F32)
    tmp[HEADS : HEADS + KVH, 0:SEL] = (ids // POOL).astype(F32)
    tmp[HEADS + KVH : SLAB, 0:SEL] = (ids % POOL).astype(F32)
    slab = tmp[...].astype(BF)
    for copy in range(SPAN):
        out_ref[copy, :, :] = slab
    copies[2].wait()
    copies[3].wait()


def halves_kernel(side_ref, w_hbm, mine_ref, given_ref, sems):
    width = mine_ref.shape[1]
    side = side_ref[0]
    mine = pl.ds(pl.multiple_of(side * width, width), width)
    given = pl.ds(pl.multiple_of((1 - side) * width, width), width)
    copies = [
        pltpu.make_async_copy(w_hbm.at[:, given], given_ref, sems.at[0]),
        pltpu.make_async_copy(w_hbm.at[:, mine], mine_ref, sems.at[1]),
    ]
    for copy in copies:
        copy.start()
    for copy in copies:
        copy.wait()


def spread_kernel(x_ref, out_ref):
    for copy in range(SPAN):
        out_ref[copy, :, :, :] = x_ref[...]


def attend_kernel(place_ref, q_ref, *refs):
    own_ref, kv_hbms = refs[0], refs[1:SHARE]
    out_ref, others, sems, qa, point, acc, s_even, s_odd = refs[SHARE:]
    copies = [
        pltpu.make_async_copy(kv_hbms[block], others.at[block], sems.at[block])
        for block in range(SHARE - 1)
    ]
    for copy in copies:
        copy.start()
    kv_refs = [own_ref] + [others.at[block] for block in range(SHARE - 1)]
    odd = place_ref[SHARE]
    ids = q_ref[:, HEADS:SLAB, :].astype(F32).reshape(OWN * 8, HD).astype(BF)
    i, j = iota((KVH * OWN, OWN * 8), 0), iota((KVH * OWN, OWN * 8), 1)
    first = (i % OWN) * 8 + i // OWN
    owner = dot(one_if(j == first), ids)
    slot = dot(one_if(j == first + KVH), ids)
    code = jnp.full((KVH * OWN, HD), -1.0, F32)
    for block in range(SHARE):
        code = jnp.where(owner == place_ref[block].astype(F32), slot + float(block * POOL), code)
    lane = iota((KVH * OWN, HD), 1).astype(F32)
    bias = jnp.full((KVH * OWN, HD), -FAR, F32)
    for j in range(SEL):
        bias = jnp.where(code[:, j : j + 1] == lane, 0.0, bias)
    bias = bias.astype(BF)
    i, j = iota((256, 256), 0), iota((256, 256), 1)
    swap = one_if((j % 16) * 16 + j // 16 == i)
    for h in range(KVH):
        for c in range(OWN // 16):
            part = q_ref[c * 16 : (c + 1) * 16, h * 16 : (h + 1) * 16, :]
            turned = dot(swap, part.reshape(256, HD)).astype(BF)
            for g in range(GROUP):
                head = h * GROUP + g
                at = jnp.where(odd == 1, head, (head % LINE) * LINE + head // LINE)
                row = pl.multiple_of(at * OWN + c * 16, 16)
                qa[pl.ds(row, 16), 0:HD] = turned[g * 16 : (g + 1) * 16, :]
                qa[pl.ds(row, 16), HD : 2 * HD] = bias[h * OWN + c * 16 : h * OWN + (c + 1) * 16, :]

    point[...] = jnp.full(point.shape, FLOOR, F32)
    acc[...] = jnp.zeros(acc.shape, F32)
    first_lane = one_if(iota((TOKENS, HD), 1) == 0)
    token_page, page_lane = iota((TOKENS, HD), 0) // PAGE, iota((TOKENS, HD), 1)

    def score(block, n):
        if (block, n) == (1, 0):
            for copy in copies:
                copy.wait()
        keys = jnp.concatenate(
            [kv_refs[block][0], one_if(page_lane == token_page + block * POOL)], axis=1
        )
        return dot_nt(qa[n * CHUNK : (n + 1) * CHUNK, :], keys)

    def finish(block, n, s_ref):
        here = slice(n * CHUNK, (n + 1) * CHUNK)
        s = s_ref[...]
        top = jnp.max(s, axis=1, keepdims=True) * SCALE
        old = point[here, :]
        new = jnp.maximum(jnp.broadcast_to(top.astype(BF).astype(F32), old.shape), old)
        point[here, :] = new
        p = jnp.exp2(s * (SCALE * LOG2E) - new[:, 0:1] * LOG2E).astype(BF)
        o = dot(p, jnp.concatenate([kv_refs[block][1], first_lane], axis=1))
        fade = jnp.exp2((old - new) * LOG2E)
        acc[here, :] = acc[here, :] * jnp.concatenate([fade, fade], axis=1) + o

    chunks = HEADS * OWN // CHUNK
    steps = [(block, n) for block in range(SHARE) for n in range(chunks)]
    slots = (s_even, s_odd)
    slots[0][...] = score(*steps[0])
    for k, step in enumerate(steps):
        if k + 1 < len(steps):
            slots[(k + 1) % 2][...] = score(*steps[k + 1])
        finish(*step, slots[k % 2])

    lane = iota((OWN, HD), 1)
    for j in range(LINE):
        stats = jnp.zeros((OWN, HD), F32)
        for i in range(LINE):
            here = slice((j * LINE + i) * OWN, (j * LINE + i + 1) * OWN)
            total = acc[here, HD : HD + 1]
            total_hi = total.astype(BF).astype(F32)
            stats = jnp.where(lane == i * 8, point[here, :], stats)
            stats = jnp.where(lane == i * 8 + 1, total_hi, stats)
            stats = jnp.where(lane == i * 8 + 2, total - total_hi, stats)
            out_ref[j, i * OWN : (i + 1) * OWN, :] = acc[here, 0:HD].astype(BF)
        out_ref[j, LINE * OWN : (LINE + 1) * OWN, :] = stats.astype(BF)


def merge_kernel(r_ref, out_ref):
    kind = iota((OWN, HD), 1) % 8
    stats_of_all = []
    for rows in range(PAIR):
        sources = range(rows, LINE, PAIR)
        stats = [r_ref[src, LINE * OWN : (LINE + 1) * OWN, :].astype(F32) for src in sources]
        top = functools.reduce(jnp.maximum, stats)
        factors = [jnp.exp2((s - top) * LOG2E) for s in stats]
        total = sum(
            f * (pltpu.roll(s, HD - 1, 1) + pltpu.roll(s, HD - 2, 1))
            for f, s in zip(factors, stats)
        )
        total_hi = total.astype(BF).astype(F32)
        total_lo = pltpu.roll(total - total_hi, 2, 1)
        joint = jnp.where(kind == 1, pltpu.roll(total_hi, 1, 1), jnp.where(kind == 2, total_lo, 0.0))
        stats_of_all.append(jnp.where(kind == 0, top, joint))
        for head in range(LINE):
            acc = sum(
                f[:, head * 8 : head * 8 + 1] * r_ref[src, head * OWN : (head + 1) * OWN, :].astype(F32)
                for f, src in zip(factors, sources)
            ).astype(BF)
            out_ref[head, 0, rows * OWN : (rows + 1) * OWN, :] = acc
            out_ref[head ^ 1, 1, rows * OWN : (rows + 1) * OWN, :] = acc
    tall = jnp.concatenate(stats_of_all + [jnp.zeros((HD - HALF, HD), F32)], axis=0).T
    for head in range(LINE):
        stats = tall[head * 8 : (head + 1) * 8, :].astype(BF)
        out_ref[head, 0, HALF:SMALL, :] = stats
        out_ref[head ^ 1, 1, HALF:SMALL, :] = stats


def project_kernel(r_ref, mine_ref, theirs_hbm, out_ref, att, theirs_ref, sem):
    copy = pltpu.make_async_copy(theirs_hbm, theirs_ref, sem)
    copy.start()
    heads = []
    for head in range(PAIR):
        halves = []
        for rows in range(PAIR):
            sources = range(rows, LINE, PAIR)
            stats = [r_ref[src, head, HALF:SMALL, :].astype(F32).T[0:HALF, :] for src in sources]
            top = functools.reduce(jnp.maximum, [s[:, 0:1] for s in stats])
            factors = [jnp.exp2((s[:, 0:1] - top) * LOG2E) for s in stats]
            total = sum(f * (s[:, 1:2] + s[:, 2:3]) for f, s in zip(factors, stats))
            acc = sum(
                f * r_ref[src, head, 0:HALF, :].astype(F32) for src, f in zip(sources, factors)
            )
            halves.append((acc / total).astype(BF))
        heads.append(jnp.concatenate(halves, axis=0))
    both = jnp.concatenate(heads, axis=1)
    i, j = iota((ROWS, ROWS), 0), iota((ROWS, ROWS), 1)
    b, u = i // LINE, i % LINE
    came_from = (b % PAIR) * HALF + (u % PAIR) * OWN + (b // PAIR) * SPAN + u // PAIR
    att[...] = dot(one_if(j == came_from), both).astype(BF)

    copy.wait()
    for n in range(out_ref.shape[1] // BLOCK):
        lanes = slice(n * BLOCK, (n + 1) * BLOCK)
        weight = jnp.concatenate([mine_ref[:, lanes], theirs_ref[:, lanes]], axis=0)
        out_ref[:, lanes] = dot(att[...], weight).astype(BF)


def add_kernel(x_ref, out_ref, tmp):
    tiles = tmp.shape[0] // LINE
    half = tiles // PAIR
    for tile in range(tiles):
        lanes = slice(tile % half * 128, (tile % half + 1) * 128)
        total = sum(x_ref[src, :, lanes].astype(F32) for src in range(tile // half, LINE, PAIR))
        tmp[pl.ds(tile, LINE, stride=tiles), :] = total
    out_ref[...] = tmp[...].reshape(LINE, tiles, 128).astype(BF)


VMEM = pl.BlockSpec(memory_space=pltpu.VMEM)
ANYWHERE = pl.BlockSpec(memory_space=pl.ANY)
SMEM = pl.BlockSpec(memory_space=pltpu.SMEM)
PARAMS = pltpu.CompilerParams(vmem_limit_bytes=24 * 2**20)


def in_hbm(value):
    return pltpu.with_memory_space_constraint(value, pltpu.HBM)


def prepare(queries, ids, keys, values):
    return pl.pallas_call(
        prepare_kernel,
        out_shape=(
            jax.ShapeDtypeStruct((SPAN, SLAB, HD), BF),
            jax.ShapeDtypeStruct((2, TOKENS, HD), BF),
        ),
        in_specs=[ANYWHERE] * 4,
        out_specs=(VMEM, VMEM),
        scratch_shapes=[
            pltpu.VMEM(queries.shape, BF),
            pltpu.VMEM(ids.shape, jnp.int32),
            pltpu.VMEM((SLAB, HD), F32),
            pltpu.SemaphoreType.DMA((4,)),
        ],
        compiler_params=PARAMS,
        name="prepare",
    )(*[in_hbm(value) for value in (queries, ids, keys, values)])


def halves(side, weight):
    half = jax.ShapeDtypeStruct((HD, weight.shape[1] // PAIR), BF)
    return pl.pallas_call(
        halves_kernel,
        out_shape=(half, half),
        in_specs=[SMEM, ANYWHERE],
        out_specs=(VMEM, VMEM),
        scratch_shapes=[pltpu.SemaphoreType.DMA((2,))],
        compiler_params=PARAMS,
        name="halves",
    )(side, in_hbm(weight))


def spread(value):
    return pl.pallas_call(
        spread_kernel,
        out_shape=jax.ShapeDtypeStruct((SPAN,) + value.shape, BF),
        in_specs=[VMEM],
        out_specs=VMEM,
        compiler_params=PARAMS,
        name="spread",
    )(value)


def attend(place, got, pages):
    return pl.pallas_call(
        attend_kernel,
        out_shape=jax.ShapeDtypeStruct((LINE, (LINE + 1) * OWN, HD), BF),
        in_specs=[SMEM, VMEM, VMEM] + [ANYWHERE] * (SHARE - 1),
        out_specs=VMEM,
        scratch_shapes=[
            pltpu.VMEM((SHARE - 1, 2, TOKENS, HD), BF),
            pltpu.SemaphoreType.DMA((SHARE - 1,)),
            pltpu.VMEM((HEADS * OWN, 2 * HD), BF),
            pltpu.VMEM((HEADS * OWN, HD), F32),
            pltpu.VMEM((HEADS * OWN, 2 * HD), F32),
            pltpu.VMEM((CHUNK, TOKENS), F32),
            pltpu.VMEM((CHUNK, TOKENS), F32),
        ],
        compiler_params=PARAMS,
        name="attend",
    )(place, got, pages[0], *[in_hbm(block) for block in pages[1:]])


def merge(parts):
    return pl.pallas_call(
        merge_kernel,
        out_shape=jax.ShapeDtypeStruct((LINE, PAIR, SMALL, HD), BF),
        in_specs=[VMEM],
        out_specs=VMEM,
        compiler_params=PARAMS,
        name="merge",
    )(parts)


def project(parts, mine, theirs):
    width = theirs.shape[1]
    return pl.pallas_call(
        project_kernel,
        out_shape=jax.ShapeDtypeStruct((ROWS, width), BF),
        in_specs=[VMEM, VMEM, ANYWHERE],
        out_specs=VMEM,
        scratch_shapes=[
            pltpu.VMEM((ROWS, PAIR * HD), BF),
            pltpu.VMEM(theirs.shape, BF),
            pltpu.SemaphoreType.DMA,
        ],
        compiler_params=PARAMS,
        name="project",
    )(parts, mine, theirs)


def add(parts):
    width = parts.shape[2] * PAIR
    return pl.pallas_call(
        add_kernel,
        out_shape=jax.ShapeDtypeStruct((LINE, width // 128, 128), BF),
        in_specs=[VMEM],
        out_specs=VMEM,
        scratch_shapes=[pltpu.VMEM((LINE * width // 128, 128), F32)],
        compiler_params=PARAMS,
        name="add",
    )(parts)


def lines(sections, first):
    groups = []
    for section in range(sections):
        base = section * LINE * LINE
        along_y = (section % 2 == 0) == first
        for other in range(LINE):
            step, start = (1, other * LINE) if along_y else (LINE, other)
            groups.append([base + start + step * k for k in range(LINE)])
    return groups


def exchange(value, groups):
    return lax.all_to_all(
        value, ("segment", "dev"), split_axis=0, concat_axis=0, axis_index_groups=groups, tiled=True
    )


def neighbours(groups):
    return [(line[k], line[k ^ 1]) for line in groups for k in range(LINE)]


def local(queries, page_ids, key_pages, value_pages, out_weight):
    count = lax.axis_size("segment")
    both = ("segment", "dev")
    one, other = lines(count, True), lines(count, False)
    one_rows = [line[rows::PAIR] for line in one for rows in range(PAIR)]
    other_rows = [line[rows::PAIR] for line in other for rows in range(PAIR)]
    odd = lax.axis_index("segment") % 2
    me = lax.axis_index("dev")
    u = jnp.where(odd == 1, me // LINE, me % LINE)
    b = jnp.where(odd == 1, me % LINE, me // LINE)
    place = []
    for block in range(SHARE):
        block_u, block_b = u ^ (block % 2), b ^ (block // 2)
        place.append(jnp.where(odd == 1, block_u * LINE + block_b, block_b * LINE + block_u))
    place = jnp.stack(place + [odd]).astype(jnp.int32)

    payload, pages = prepare(
        queries,
        page_ids.reshape(KVH, SEL),
        key_pages.reshape(TOKENS, HD),
        value_pages.reshape(TOKENS, HD),
    )
    mine, given = halves((b % PAIR).astype(jnp.int32).reshape(1), out_weight)
    near = exchange(payload, one_rows)
    pages_u = lax.ppermute(pages, both, neighbours(one))
    pages_b = lax.ppermute(pages, both, neighbours(other))
    near, came_u, _, given = lax.optimization_barrier((near, pages_u, pages_b, given))
    pages_ub = lax.ppermute(came_u, both, neighbours(other))
    got = exchange(spread(near), other_rows)
    given, got, _ = lax.optimization_barrier((given, got, pages_ub))

    partial = attend(place, got.reshape(OWN, SLAB, HD), [pages, pages_u, pages_b, pages_ub])
    given, partial = lax.optimization_barrier((given, partial))
    theirs = lax.ppermute(given, both, neighbours(other))
    joined = merge(exchange(partial, one))
    gathered = exchange(joined, other)
    sums = project(gathered, mine, theirs)
    added = add(exchange(sums.reshape(LINE, LINE, -1), other))
    parts = exchange(added, one)
    projected = jnp.sum(parts.astype(F32), axis=0).astype(BF)
    handed = lax.ppermute(projected, "segment", [(s, (s + 1) % count) for s in range(count)])
    return handed.reshape(1, -1)


def solution(mesh):
    placed = (
        P(("segment", "dev"), None),
        P(("segment", "dev"), None, None),
        P(("segment", "dev"), None, None),
        P(("segment", "dev"), None, None),
        P(("segment", "dev"), None),
    )
    return jax.shard_map(
        local, mesh=mesh, in_specs=placed, out_specs=P(("segment", "dev"), None), check_vma=False
    )
```
